32 devices in a mesh: seq: 4 (over z), clus: 8 (over y, x, core).
Axes of the slice: x: 2, y: 2, z: 4, core: 2. Of those that a mesh axis runs over, the one named last changes fastest.
Arguments:
- node_feats: bfloat16 [8, 512, 1024], P('clus', 'seq'), may hold values from -24 to 24
- qkv_weight: bfloat16 [3072, 1024], P('seq'), may hold values from -1 to 1
- block_pairs: int32 [8, 8, 2], P('clus'), may hold values from 0 to 3, as said below
- grad_out: bfloat16 [8, 512, 1024], P('clus', 'seq'), may hold values from -6 to 6
Outputs:
- attended: bfloat16 [8, 512, 1024], P('clus', 'seq')
- node_grad: bfloat16 [8, 512, 1024], P('clus', 'seq')
- weight_grad: float32 [3072, 1024], P('seq')
The draws below stay inside these ranges and needn't reach their ends.
Inputs may be any that keep to these rules, and one draw needn't show every extreme that they name: `block_pairs`: each cluster's list holds 8 distinct pairs, among them (b, b) for every block b.
All inputs are finite; a program needn't handle non-finite values.
Results may differ from the reference program's by a relative error of at most 0.023.
Values may be sent and summed in bfloat16 or wider, within the bound.
No kernel may reach another device: no remote copies, remote signals or barrier semaphores. Data moves between devices by JAX's collectives and lax.ppermute only.
A program may use at most 64 MiB of HBM per device.

```python
import jax
import jax.numpy as jnp
from jax import lax

D = 1024
H = 16
HD = 64
BLOCK = 128
NODES = 512
CLUSTERS = 8
NB = 4
PAIRS = 8
N_SEQ = 4
N_CLUS = 8


def draw_node_feats(key, part):
    key_base = jax.random.fold_in(key, 0)
    return jnp.clip(jax.random.normal(key_base, (CLUSTERS, NODES, D), jnp.float32), -5.0, 5.0).astype(jnp.bfloat16)


def draw_qkv_weight(key, part):
    key_query, key_keys, key_values = jax.random.split(key, 3)
    shape_one = (D, H, 1, HD)
    query_part = jnp.clip(jax.random.normal(key_query, shape_one, jnp.float32), -4.0, 4.0) / D ** 0.5
    keys_part = jnp.clip(jax.random.normal(key_keys, shape_one, jnp.float32), -4.0, 4.0) / D ** 0.5
    values_part = jnp.clip(jax.random.normal(key_values, shape_one, jnp.float32), -4.0, 4.0) / D ** 0.5
    return jnp.concatenate([query_part, keys_part, values_part], axis=2).reshape(D, 3 * D).T.astype(jnp.bfloat16)


def draw_block_pairs(key, part):

    def one_cluster(cluster_key):
        key_noise, key_skew, key_order = jax.random.split(cluster_key, 3)
        random_part = jax.random.randint(key_noise, (NB, NB), 0, 16384)
        skewed = jax.random.randint(key_skew, (NB, 1), 0, 4) * 8192
        position = jnp.arange(NB * NB, dtype=jnp.int32).reshape(NB, NB)
        ranking = (random_part + skewed) * 32768 + position
        diagonal = jnp.arange(NB)[:, None] == jnp.arange(NB)[None, :]
        ranking = jnp.where(diagonal, -1, ranking).reshape(-1)
        chosen = lax.top_k(ranking, PAIRS - NB)[1].astype(jnp.int32)
        rows_all = jnp.concatenate([jnp.arange(NB, dtype=jnp.int32), chosen // NB])
        cols_all = jnp.concatenate([jnp.arange(NB, dtype=jnp.int32), chosen % NB])
        listed = jnp.stack([rows_all, cols_all], axis=1)
        shuffle = jax.random.permutation(key_order, PAIRS)
        return listed[shuffle]
    return jax.vmap(one_cluster)(jax.random.split(key, CLUSTERS))


def steps_of(stream_key, extent, shards, low, high):
    def one(dim, parts):
        heights = jax.random.uniform(jax.random.fold_in(jax.random.fold_in(stream_key, 6), dim), (parts,), jnp.float32, low / len(shards), high / len(shards))
        return jnp.repeat(jnp.exp(heights), extent[dim] // parts).reshape((-1,) + (1,) * (len(extent) - dim - 1))

    loudness = one(*shards[0])
    for cut in shards[1:]:
        loudness = loudness * one(*cut)
    return loudness


def normal_values(key, dims, spread, limit, cuts=(), held_as=jnp.bfloat16):
    drawn = jax.random.normal(key, dims, jnp.float32) * spread
    if len(cuts) > 0:
        drawn = steps_of(key, dims, cuts, -0.22, 0.18) * drawn
    return jnp.clip(drawn, min=-limit, max=limit).astype(held_as)


def setup_inputs(seed: int = 0) -> dict:
    splits = jax.random.split(jax.random.key(seed), 5)
    node_feats = draw_node_feats(jax.random.fold_in(splits[4], 71), 0)
    qkv_weight = draw_qkv_weight(jax.random.fold_in(splits[4], 71), 0)
    block_pairs = draw_block_pairs(jax.random.fold_in(splits[4], 71), 0)
    grad_out = normal_values(splits[3], (CLUSTERS, NODES, D), 1.0, 6.0, ((0, 8), (1, 4)))
    return {"node_feats": node_feats, "qkv_weight": qkv_weight, "block_pairs": block_pairs, "grad_out": grad_out}


def block_allowed(listed, blocks):
    block_ids = jnp.arange(blocks, dtype=jnp.int32)[None, :]
    row_hot = (listed[:, 0:1] == block_ids).astype(jnp.float32)
    col_hot = (listed[:, 1:2] == block_ids).astype(jnp.float32)
    counts = jnp.dot(row_hot.T, col_hot, precision=lax.Precision.HIGHEST)
    return counts > 0.5


def one_head(projected, upstream, allowed, head_index):
    node_count = projected.shape[0]
    grouped = projected.reshape(node_count, H, 3, HD)
    chosen = lax.dynamic_index_in_dim(grouped, head_index, 1, keepdims=False)
    queries = chosen[:, 0]
    keys_all = chosen[:, 1]
    values_all = chosen[:, 2]
    grad_rows = lax.dynamic_index_in_dim(upstream.reshape(node_count, H, HD), head_index, 1, keepdims=False)
    scores = jnp.dot(queries, keys_all.T, preferred_element_type=jnp.float32) * (HD ** -0.5)
    scores = jnp.where(allowed, scores, -jnp.inf)
    row_max = jnp.max(scores, axis=-1, keepdims=True)
    unnorm = jnp.where(allowed, jnp.exp(scores - row_max), 0.0)
    weights = unnorm / jnp.sum(unnorm, axis=-1, keepdims=True)
    weights_low = weights.astype(jnp.bfloat16)
    head_out = jnp.dot(weights_low, values_all, preferred_element_type=jnp.float32).astype(jnp.bfloat16)
    grad_weights = jnp.dot(grad_rows, values_all.T, preferred_element_type=jnp.float32)
    row_delta = jnp.sum(weights * grad_weights, axis=-1, keepdims=True)
    grad_scores = (weights * (grad_weights - row_delta) * (HD ** -0.5)).astype(jnp.bfloat16)
    grad_query = jnp.dot(grad_scores, keys_all, preferred_element_type=jnp.float32).astype(jnp.bfloat16)
    grad_keys = jnp.dot(grad_scores.T, queries, preferred_element_type=jnp.float32).astype(jnp.bfloat16)
    grad_values = jnp.dot(weights_low.T, grad_rows, preferred_element_type=jnp.float32).astype(jnp.bfloat16)
    return head_out, jnp.stack([grad_query, grad_keys, grad_values], axis=1)


def reference(node_feats, qkv_weight, block_pairs, grad_out):
    def one_cluster(running, inputs):
        features, listed, upstream = inputs
        node_count = features.shape[0]
        projected = lax.dot_general(features, qkv_weight, (((1,), (1,)), ((), ())), preferred_element_type=jnp.float32).astype(jnp.bfloat16)
        allowed_blocks = block_allowed(listed, node_count // BLOCK)
        allowed = jnp.repeat(jnp.repeat(allowed_blocks, BLOCK, axis=0), BLOCK, axis=1)
        heads_out, head_grads = lax.map(lambda head_index: one_head(projected, upstream, allowed, head_index), jnp.arange(H))
        attended = jnp.transpose(heads_out, (1, 0, 2)).reshape(node_count, D)
        grad_proj = jnp.transpose(head_grads, (1, 0, 2, 3)).reshape(node_count, 3 * D)
        group_cols = 3 * D // N_SEQ
        summed = jnp.zeros((node_count, D), jnp.float32)
        for group_index in range(N_SEQ):
            lower = group_index * group_cols
            upper = lower + group_cols
            group_term = jnp.dot(grad_proj[:, lower:upper], qkv_weight[lower:upper, :], preferred_element_type=jnp.float32).astype(jnp.bfloat16)
            summed = summed + lax.optimization_barrier(group_term).astype(jnp.float32)
        node_grad = summed.astype(jnp.bfloat16)
        running = running + lax.dot_general(grad_proj, features, (((0,), (0,)), ((), ())), preferred_element_type=jnp.float32)
        return running, (attended, node_grad)

    initial = jnp.zeros((3 * D, D), jnp.float32)
    summed_w, outputs = lax.scan(one_cluster, initial, (node_feats, block_pairs, grad_out))
    return outputs[0], outputs[1], summed_w / N_CLUS
```

```python
import functools

import jax
import jax.numpy as jnp
from jax import lax
from jax.experimental import pallas as pl
from jax.experimental.pallas import tpu as pltpu
from jax.sharding import PartitionSpec as P

HD = 64
BLOCK = 128
F32 = jnp.float32
BF16 = jnp.bfloat16
NT = (((1,), (1,)), ((), ()))
TN = (((0,), (0,)), ((), ()))
VMEM = pl.BlockSpec(memory_space=pltpu.VMEM)
SMEM = pl.BlockSpec(memory_space=pltpu.SMEM)


def mm(a, b, dims=(((1,), (0,)), ((), ()))):
    return lax.dot_general(a, b, dims, preferred_element_type=F32)


class Plan:
    def __init__(self, rows, columns, n):
        self.n, self.rows, self.columns = n, rows, columns
        self.nodes = n * rows
        self.heads = columns // (3 * HD)
        self.groups = 2 if self.heads % 2 == 0 else 1
        self.gheads = self.heads // self.groups
        self.per_tile = 2 if self.gheads % 2 == 0 else 1
        self.tiles = self.gheads // self.per_tile
        self.tile = self.per_tile * HD
        self.gcols = self.gheads * 3 * HD
        self.chunk = BLOCK


def attend_group(plan, group, qkv, grads, bias, out_ref, grad_ref, scratch):
    q_s, k_s, v_s, g_s, p_s, ds_s = scratch
    rows, tile, chunk = plan.rows, plan.tile, plan.chunk
    lane = lax.broadcasted_iota(jnp.int32, (1, tile), 1)
    for t in range(plan.tiles):
        base = group * plan.gcols + t * 3 * tile
        gbase = (group * plan.tiles + t) * tile
        if plan.groups > 1:
            base, gbase = pl.multiple_of(base, tile), pl.multiple_of(gbase, tile)
        for s in range(plan.n):
            here = slice(s * rows, (s + 1) * rows)
            q_s[here, :] = qkv[s][:, pl.ds(base, tile)]
            k_s[here, :] = qkv[s][:, pl.ds(base + tile, tile)]
            v_s[here, :] = qkv[s][:, pl.ds(base + 2 * tile, tile)]
            g_s[here, :] = grads[s][:, pl.ds(gbase, tile)]
        grad_keys = grad_values = None
        for h in range(plan.per_tile):
            mine = (lane >= h * HD) & (lane < (h + 1) * HD)

            def only(x):
                return jnp.where(mine, x, jnp.zeros_like(x))

            def one_chunk(i, carry):
                lo = i * chunk if isinstance(i, int) else pl.multiple_of(i * chunk, chunk)
                here = pl.ds(lo, chunk)
                scores = mm(only(q_s[here, :]), k_s[...], NT) * HD ** -0.5
                scores = scores + bias[pl.ds(i, 1), :]
                unnorm = jnp.exp(scores - jnp.max(scores, axis=-1, keepdims=True))
                weights = unnorm / jnp.sum(unnorm, axis=-1, keepdims=True)
                low = weights.astype(BF16)
                out = mm(low, v_s[...])
                grad_weights = mm(only(g_s[here, :]), v_s[...], NT)
                delta = jnp.sum(weights * grad_weights, axis=-1, keepdims=True)
                ds = (weights * (grad_weights - delta) * HD ** -0.5).astype(BF16)
                grad_q = mm(ds, k_s[...])
                p_s[here, :] = low
                ds_s[here, :] = ds
                out, grad_q = out.astype(BF16), grad_q.astype(BF16)
                if h > 0:
                    out = jnp.where(mine, out, out_ref[here, t * tile : (t + 1) * tile])
                    grad_q = jnp.where(
                        mine, grad_q, grad_ref[here, 3 * t * tile : (3 * t + 1) * tile]
                    )
                out_ref[here, t * tile : (t + 1) * tile] = out
                grad_ref[here, 3 * t * tile : (3 * t + 1) * tile] = grad_q
                return carry

            steps = plan.nodes // chunk
            if steps <= 4:
                for i in range(steps):
                    one_chunk(i, 0)
            else:
                lax.fori_loop(0, steps, one_chunk, 0)
            gk = mm(ds_s[...], q_s[...], TN)
            gv = mm(p_s[...], g_s[...], TN)
            grad_keys = gk if h == 0 else jnp.where(mine, gk, grad_keys)
            grad_values = gv if h == 0 else jnp.where(mine, gv, grad_values)
        grad_ref[:, (3 * t + 1) * tile : (3 * t + 2) * tile] = grad_keys.astype(BF16)
        grad_ref[:, (3 * t + 2) * tile : (3 * t + 3) * tile] = grad_values.astype(BF16)


def first_kernel(plan, *refs):
    n = plan.n
    which, qkv, grads, feats = refs[0], refs[1 : 1 + n], refs[1 + n : 1 + 2 * n], refs[1 + 2 * n : 1 + 3 * n]
    bias = refs[1 + 3 * n]
    out_ref, grad_ref, wgrad_ref = refs[2 + 3 * n : 5 + 3 * n]
    scratch = refs[5 + 3 * n :]
    attend_group(plan, which[0], qkv, grads, bias, out_ref, grad_ref, scratch[:6])
    full = scratch[6]
    for s in range(n):
        full[s * plan.rows : (s + 1) * plan.rows, :] = feats[s][...]
    wgrad_ref[...] = mm(grad_ref[...], full[...], TN).astype(BF16)


def second_kernel(plan, *refs):
    n, rows = plan.n, plan.rows
    which, qkv, grads, feats = refs[0], refs[1 : 1 + n], refs[1 + n : 1 + 2 * n], refs[1 + 2 * n : 1 + 3 * n]
    bias, weight = refs[1 + 3 * n : 3 + 3 * n]
    at = 3 + 3 * n
    if plan.groups > 1:
        out_other, grad_other = refs[at : at + 2]
        at += 2
    terms, outs = refs[at : at + n], refs[at + n : at + 2 * n]
    wgrad_ref = refs[at + 2 * n]
    scratch = refs[at + 2 * n + 1 :]
    full, out_ref, grad_ref = scratch[6:9]
    group = which[0] if plan.groups > 1 else 0
    attend_group(plan, group, qkv, grads, bias, out_ref, grad_ref, scratch[:6])
    for s in range(n):
        here = slice(s * rows, (s + 1) * rows)
        full[here, :] = feats[s][...]
        if plan.groups > 1:
            width = plan.gheads * HD
            outs[s][:, pl.ds(pl.multiple_of(group * width, width), width)] = out_ref[here, :]
            other = 1 - group
            outs[s][:, pl.ds(pl.multiple_of(other * width, width), width)] = out_other[here, :]
            gcols = plan.gcols
            term = mm(grad_ref[here, :], weight[pl.ds(pl.multiple_of(group * gcols, gcols), gcols), :])
            term = term + mm(
                grad_other[here, :], weight[pl.ds(pl.multiple_of(other * gcols, gcols), gcols), :]
            )
        else:
            outs[s][...] = out_ref[here, :]
            term = mm(grad_ref[here, :], weight[...])
        terms[s][...] = term.astype(BF16)
    wgrad_ref[...] = mm(grad_ref[...], full[...], TN)


def call(kernel, plan, out_shape, scratch, count, args):
    return pl.pallas_call(
        functools.partial(kernel, plan),
        out_shape=out_shape,
        in_specs=[SMEM] + [VMEM] * (len(args) - 1),
        out_specs=[VMEM] * len(out_shape),
        scratch_shapes=scratch,
        compiler_params=pltpu.CompilerParams(vmem_limit_bytes=50 * 2**20),
        cost_estimate=pl.CostEstimate(flops=count, bytes_accessed=4 << 20, transcendentals=0),
    )(*args)


def swap(x, axis, bits):
    size = lax.axis_size(axis)
    return lax.ppermute(x, axis, [(i, i ^ bits) for i in range(size)])


def add(a, b):
    return (a.astype(F32) + b.astype(F32)).astype(BF16)


def gather_slots(x, z, n):
    if n != 4:
        return [x] + [swap(x, "seq", k) for k in range(1, n)]
    far = swap(x, "seq", 2)
    near = swap(x, "seq", 1)
    middle = lax.ppermute(x, "seq", [(1, 2), (2, 1)])
    ends = lax.ppermute(far, "seq", [(2, 3), (1, 0)])
    inner = (z == 1) | (z == 2)
    return [x, near, far, jnp.where(inner, middle, ends)]


def reduce_slots(terms, z, n):
    if n != 4:
        total = terms[0].astype(F32)
        for k in range(1, n):
            total = total + swap(terms[k], "seq", k).astype(F32)
        return total.astype(BF16)
    inner = (z == 1) | (z == 2)
    ends = lax.ppermute(terms[3], "seq", [(3, 2), (0, 1)])
    middle = lax.ppermute(terms[3], "seq", [(1, 2), (2, 1)])
    near = swap(terms[1], "seq", 1)
    far = swap(jnp.where(inner, add(terms[2], ends), terms[2]), "seq", 2)
    total = terms[0].astype(F32) + near.astype(F32) + far.astype(F32)
    return jnp.where(inner, total + middle.astype(F32), total).astype(BF16)


def sum_pairs(x, bits):
    return add(x, swap(x, "clus", bits))


def local(node_feats, qkv_weight, block_pairs, grad_out):
    feats = node_feats[0]
    rows, width = feats.shape
    n, m = lax.axis_size("seq"), lax.axis_size("clus")
    z, c = lax.axis_index("seq"), lax.axis_index("clus")
    plan = Plan(rows, qkv_weight.shape[0], n)
    nodes, heads = plan.nodes, plan.heads
    core = c % 2

    xs = gather_slots(feats, z, n)
    hcols = heads * HD

    def for_slot(k):
        return lax.dynamic_slice_in_dim(grad_out[0], (z ^ k) * hcols, hcols, 1)

    grads = [for_slot(0)] + [swap(for_slot(k), "seq", k) for k in range(1, n)]

    grouped = (plan.groups, plan.tiles, plan.per_tile, 3, HD, width)
    weight = qkv_weight.reshape(grouped).transpose(0, 1, 3, 2, 4, 5).reshape(plan.columns, width)
    qkv = [mm(x, weight, NT).astype(BF16) for x in xs]

    per_dev = rows // BLOCK
    blocks = nodes // BLOCK
    listed = block_pairs[0]
    place = ((listed // per_dev) ^ z) * per_dev + listed % per_dev
    ids = jnp.arange(blocks, dtype=jnp.int32)
    row_hot = place[:, 0, None, None] == ids[None, :, None]
    col_hot = place[:, 1, None, None] == ids[None, None, :]
    allowed = jnp.any(row_hot & col_hot, axis=0)
    bias = jnp.where(jnp.repeat(allowed, BLOCK, axis=1), 0.0, -jnp.inf).astype(F32)

    flops = 14 * nodes * nodes * HD * plan.gheads + 4 * nodes * plan.gcols * width
    tile_scratch = [pltpu.VMEM((nodes, plan.tile), BF16)] * 4 + [pltpu.VMEM((nodes, nodes), BF16)] * 2
    full = [pltpu.VMEM((nodes, width), BF16)]
    common = [*qkv, *grads, *xs, bias]
    other = []
    if plan.groups > 1:
        out_other, grad_other, wgrad_other = call(
            first_kernel,
            plan,
            [
                jax.ShapeDtypeStruct((nodes, plan.gheads * HD), BF16),
                jax.ShapeDtypeStruct((nodes, plan.gcols), BF16),
                jax.ShapeDtypeStruct((plan.gcols, width), BF16),
            ],
            tile_scratch + full,
            flops,
            [(1 - core).reshape(1), *common],
        )
        other = [out_other, grad_other]
    results = call(
        second_kernel,
        plan,
        [jax.ShapeDtypeStruct((rows, width), BF16)] * n
        + [jax.ShapeDtypeStruct((rows, hcols), BF16)] * n
        + [jax.ShapeDtypeStruct((plan.gcols, width), F32)],
        tile_scratch
        + full
        + [pltpu.VMEM((nodes, plan.gheads * HD), BF16), pltpu.VMEM((nodes, plan.gcols), BF16)],
        flops,
        [core.reshape(1), *common, weight, *other],
    )
    terms, outs, wgrad = results[:n], results[n : 2 * n], results[2 * n]

    if plan.groups > 1:
        part = add(wgrad, swap(wgrad_other, "clus", 1))
    else:
        half = plan.gcols // 2
        keep = lax.dynamic_slice_in_dim(wgrad, core * half, half, 0)
        send = lax.dynamic_slice_in_dim(wgrad, (1 - core) * half, half, 0)
        part = add(keep, swap(send.astype(BF16), "clus", 1))
    half = part.shape[0] // 2
    bits = []
    while 2 << len(bits) < m:
        bits.append(2 << len(bits))
    lower, upper = part[:half], part[half:]
    for one, two in zip(bits, bits[::-1]):
        lower, upper = sum_pairs(lower, one), sum_pairs(upper, two)
    part = jnp.concatenate([lower, upper], axis=0)
    got = swap(part, "clus", 1)
    both = jnp.where(core == 0, jnp.stack([part, got]), jnp.stack([got, part]))
    ungrouped = (plan.groups, plan.tiles, 3, plan.per_tile, HD, width)
    weight_grad = both.reshape(ungrouped).transpose(0, 1, 3, 2, 4, 5).reshape(plan.columns, width)
    weight_grad = weight_grad.astype(F32) / m

    node_grad = reduce_slots(terms, z, n)

    pieces = [outs[0]] + [swap(outs[k], "seq", k) for k in range(1, n)]
    attended = jnp.zeros((rows, n * hcols), BF16)
    for k in range(n):
        attended = lax.dynamic_update_slice_in_dim(attended, pieces[k], (z ^ k) * hcols, 1)
    return (attended[None], node_grad[None], weight_grad)


def solution(mesh):
    return jax.shard_map(
        local,
        mesh=mesh,
        in_specs=(
            P("clus", "seq", None),
            P("seq", None),
            P("clus", None, None),
            P("clus", "seq", None),
        ),
        out_specs=(P("clus", "seq", None), P("clus", "seq", None), P("seq", None)),
        check_vma=False,
    )
```

```python
import functools

import jax
import jax.numpy as jnp
from jax import lax
from jax.experimental import pallas as pl
from jax.experimental.pallas import tpu as pltpu
from jax.sharding import PartitionSpec as P

HD = 64
BLOCK = 128
F32 = jnp.float32
BF16 = jnp.bfloat16
NT = (((1,), (1,)), ((), ()))
TN = (((0,), (0,)), ((), ()))
NEVER = -1e30
VMEM = pl.BlockSpec(memory_space=pltpu.VMEM)
SMEM = pl.BlockSpec(memory_space=pltpu.SMEM)


def mm(a, b, dims=(((1,), (0,)), ((), ()))):
    return lax.dot_general(a, b, dims, preferred_element_type=F32)


class Plan:
    def __init__(self, rows, columns, n):
        self.n, self.rows, self.columns = n, rows, columns
        self.nodes = n * rows
        self.heads = columns // (3 * HD)
        self.groups = 2 if self.heads % 2 == 0 else 1
        self.gheads = self.heads // self.groups
        self.pair = self.gheads % 2 == 0
        self.per_tile = 2 if self.pair else 1
        self.tiles = self.gheads // self.per_tile
        self.tile = self.per_tile * HD
        self.gcols = self.gheads * 3 * HD
        self.chunk = BLOCK

    def base(self, group, t):
        start = group * self.gcols + t * 3 * self.tile
        return start if isinstance(start, int) else pl.multiple_of(start, self.tile)

    def feature(self, group, t):
        start = (group * self.tiles + t) * self.tile
        return start if isinstance(start, int) else pl.multiple_of(start, self.tile)


def low_half(shape):
    return lax.broadcasted_iota(jnp.int32, shape, 1) % (2 * HD) < HD


def load_tile(plan, qkv, group, t, q_s, k_s, v_s):
    base, tile = plan.base(group, t), plan.tile
    for s in range(plan.n):
        here = slice(s * plan.rows, (s + 1) * plan.rows)
        first, second, third = (qkv[s][:, pl.ds(base + i * tile, tile)] for i in range(3))
        if plan.pair:
            low = low_half(first.shape)
            queries = jnp.where(low, first, second)
            keys = pltpu.roll(jnp.where(low, third, first).astype(F32), HD, 1).astype(BF16)
            values = jnp.where(low, second, third)
        else:
            queries, keys, values = first, second, third
        q_s[here, :] = (queries.astype(F32) * HD ** -0.5).astype(BF16)
        k_s[here, :] = keys
        v_s[here, :] = values


def with_lanes(plan, h, x, extra):
    if not plan.pair:
        return jnp.concatenate([x, extra[:, :HD]], axis=1)
    low = low_half(x.shape)
    return jnp.where(low if h == 0 else ~low, x, extra)


def only_head(plan, h, x):
    if not plan.pair:
        return x
    low = low_half(x.shape)
    return jnp.where(low if h == 0 else ~low, x, jnp.zeros_like(x))


def merge(plan, h, x, before):
    if not plan.pair or h == 0:
        return x
    return jnp.where(low_half(x.shape), before, x)


def chunks(plan, body):
    steps = plan.nodes // plan.chunk
    if steps <= 4:
        for i in range(steps):
            body(i * plan.chunk)
    else:
        def step(i, carry):
            body(pl.multiple_of(i * plan.chunk, plan.chunk))
            return carry

        lax.fori_loop(0, steps, step, 0)


def forward_kernel(plan, *refs):
    n, rows = plan.n, plan.rows
    qkv, feats = refs[:n], refs[n : 2 * n]
    key_bias, row_hot = refs[2 * n : 2 * n + 2]
    at = 2 * n + 2
    outs = refs[at : at + n]
    low_ref, sum_ref, full_ref = refs[at + n : at + n + 3]
    q_s, k_s, v_s, ka_s = refs[at + n + 3 :]
    for s in range(n):
        full_ref[s * rows : (s + 1) * rows, :] = feats[s][...]
    for group in range(plan.groups):
        for t in range(plan.tiles):
            load_tile(plan, qkv, group, t, q_s, k_s, v_s)
            lanes = slice(plan.feature(group, t), plan.feature(group, t) + plan.tile)
            for h in range(plan.per_tile):
                head = (group * plan.tiles + t) * plan.per_tile + h
                ka_s[...] = with_lanes(plan, h, k_s[...], key_bias[...])

                def one_chunk(lo):
                    here = pl.ds(lo, plan.chunk)
                    queries = with_lanes(plan, h, q_s[here, :], row_hot[here, :])
                    scores = mm(queries, ka_s[...], NT)
                    unnorm = jnp.exp(scores - jnp.max(scores, axis=-1, keepdims=True))
                    low = (unnorm * (1.0 / jnp.sum(unnorm, axis=-1, keepdims=True))).astype(BF16)
                    low_ref[head, here, :] = low
                    sum_ref[here, lanes] = merge(plan, h, mm(low, v_s[...]), sum_ref[here, lanes])

                chunks(plan, one_chunk)
    for s in range(n):
        outs[s][...] = sum_ref[s * rows : (s + 1) * rows, :].astype(BF16)


def backward_kernel(plan, with_weight, *refs):
    n, rows, tile = plan.n, plan.rows, plan.tile
    group = refs[0][0] if plan.groups > 1 else 0
    qkv, grads = refs[1 : 1 + n], refs[1 + n : 1 + 2 * n]
    low_ref, sum_ref = refs[1 + 2 * n : 3 + 2 * n]
    at = 3 + 2 * n
    if with_weight:
        full_ref = refs[at]
        at += 1
    grad_ref = refs[at]
    at += 1
    if with_weight:
        wgrad_ref = refs[at]
        at += 1
    q_s, k_s, v_s, g_s, ds_s, dq_s = refs[at:]
    for t in range(plan.tiles):
        load_tile(plan, qkv, group, t, q_s, k_s, v_s)
        feature = plan.feature(group, t)
        for s in range(n):
            g_s[s * rows : (s + 1) * rows, :] = grads[s][:, pl.ds(feature, tile)]
        k_s[...] = (k_s[...].astype(F32) * HD ** -0.5).astype(BF16)
        q_t = q_s[...].T
        g_t = g_s[...].T
        for h in range(plan.per_tile):
            head = (group * plan.tiles + t) * plan.per_tile + h

            def one_chunk(lo):
                here = pl.ds(lo, plan.chunk)
                g_here = only_head(plan, h, g_s[here, :])
                delta = jnp.sum(
                    g_here.astype(F32) * sum_ref[here, pl.ds(feature, tile)], axis=-1, keepdims=True
                )
                grad_weights = mm(g_here, v_s[...], NT)
                ds = (low_ref[head, here, :].astype(F32) * (grad_weights - delta)).astype(BF16)
                ds_s[here, :] = ds
                dq_s[here, :] = merge(plan, h, mm(ds, k_s[...]), dq_s[here, :])

            chunks(plan, one_chunk)
            row = (t * plan.per_tile + h) * 3 * HD
            own = slice(h * HD, (h + 1) * HD)
            grad_ref[row + HD : row + 2 * HD, :] = mm(q_t[own, :], ds_s[...]).astype(BF16)
            grad_ref[row + 2 * HD : row + 3 * HD, :] = mm(g_t[own, :], low_ref[head]).astype(BF16)
        dq_t = dq_s[...].T.astype(BF16)
        for h in range(plan.per_tile):
            row = (t * plan.per_tile + h) * 3 * HD
            grad_ref[row : row + HD, :] = dq_t[h * HD : (h + 1) * HD, :]
    if with_weight:
        wgrad_ref[...] = mm(grad_ref[...], full_ref[...]).astype(BF16)


def weight_kernel(plan, grad_ref, full_ref, got_ref, lower_ref, upper_ref):
    half = lower_ref.shape[0]
    for i, out in enumerate((lower_ref, upper_ref)):
        here = slice(i * half, (i + 1) * half)
        out[...] = (mm(grad_ref[here, :], full_ref[...]) + got_ref[here, :].astype(F32)).astype(BF16)


def whole_weight_kernel(plan, grad_ref, full_ref, wgrad_ref):
    wgrad_ref[...] = mm(grad_ref[...], full_ref[...]).astype(BF16)


def term_kernel(plan, *refs):
    which, weight = refs[:2]
    grads = refs[2 : 2 + plan.groups]
    terms = refs[2 + plan.groups :]
    for s in range(plan.n):
        here = slice(s * plan.rows, (s + 1) * plan.rows)
        total = None
        for i, grad in enumerate(grads):
            if plan.groups > 1:
                group = which[0] if i == 0 else 1 - which[0]
                here_w = pl.ds(pl.multiple_of(group * plan.gcols, plan.gcols), plan.gcols)
            else:
                here_w = slice(None)
            part = mm(grad[:, here], weight[here_w, :], TN)
            total = part if total is None else total + part
        terms[s][...] = total.astype(BF16)


def call(kernel, plan, out_shape, scratch, flops, args, scalar=False):
    return pl.pallas_call(
        functools.partial(kernel, plan),
        out_shape=out_shape,
        in_specs=[SMEM if scalar and i == 0 else VMEM for i in range(len(args))],
        out_specs=[VMEM] * len(out_shape),
        scratch_shapes=scratch,
        compiler_params=pltpu.CompilerParams(vmem_limit_bytes=50 * 2**20),
        cost_estimate=pl.CostEstimate(flops=flops, bytes_accessed=4 << 20, transcendentals=0),
    )(*args)


def array(*shape, dtype=BF16):
    return jax.ShapeDtypeStruct(shape, dtype)


def swap(x, axis, bits):
    size = lax.axis_size(axis)
    return lax.ppermute(x, axis, [(i, i ^ bits) for i in range(size)])


def after(x, *done):
    return lax.optimization_barrier((x, *done))[0]


def add(a, b):
    return (a.astype(F32) + b.astype(F32)).astype(BF16)


def gather_slots(x, z, n):
    if n != 4:
        return [x] + [swap(x, "seq", k) for k in range(1, n)]
    far = swap(x, "seq", 2)
    near = swap(x, "seq", 1)
    ends = lax.ppermute(far, "seq", [(2, 3), (1, 0)])
    middle = lax.ppermute(after(x, far), "seq", [(1, 2), (2, 1)])
    inner = (z == 1) | (z == 2)
    return [x, near, far, jnp.where(inner, middle, ends)]


def reduce_slots(terms, z, n):
    if n != 4:
        total = terms[0].astype(F32)
        for k in range(1, n):
            total = total + swap(terms[k], "seq", k).astype(F32)
        return total.astype(BF16), terms[0]
    inner = (z == 1) | (z == 2)
    ends = lax.ppermute(terms[3], "seq", [(3, 2), (0, 1)])
    middle = lax.ppermute(terms[3], "seq", [(1, 2), (2, 1)])
    near = swap(after(terms[1], ends), "seq", 1)
    far = swap(jnp.where(inner, add(terms[2], ends), terms[2]), "seq", 2)
    total = terms[0].astype(F32) + near.astype(F32) + far.astype(F32)
    return jnp.where(inner, total + middle.astype(F32), total).astype(BF16), ends


def sum_pairs(x, bits):
    return add(x, swap(x, "clus", bits))


def local(node_feats, qkv_weight, block_pairs, grad_out):
    feats = node_feats[0]
    rows, width = feats.shape
    n, m = lax.axis_size("seq"), lax.axis_size("clus")
    z, c = lax.axis_index("seq"), lax.axis_index("clus")
    plan = Plan(rows, qkv_weight.shape[0], n)
    nodes, heads = plan.nodes, plan.heads
    core = c % 2

    xs = gather_slots(feats, z, n)
    hcols = heads * HD

    def for_slot(k):
        return lax.dynamic_slice_in_dim(grad_out[0], (z ^ k) * hcols, hcols, 1)

    own, *sent = after([for_slot(k) for k in range(n)], *xs[1:3])
    grads = [own] + [swap(sent[k - 1], "seq", k) for k in range(1, n)]

    qkv = [mm(x, qkv_weight, NT).astype(BF16) for x in xs]

    per_dev = rows // BLOCK
    blocks = nodes // BLOCK
    listed = block_pairs[0]
    place = ((listed // per_dev) ^ z) * per_dev + listed % per_dev
    ids = jnp.arange(blocks, dtype=jnp.int32)
    row_ids = jnp.arange(2 * HD, dtype=jnp.int32) % HD
    allowed = jnp.any(
        (place[:, 0, None, None] == row_ids) & (place[:, 1, None, None] == ids[:, None]), axis=0
    )
    blocked = ~allowed & (row_ids < blocks)
    key_bias = jnp.repeat(jnp.where(blocked, NEVER, 0.0).astype(BF16), BLOCK, axis=0)
    row_hot = (jnp.arange(nodes, dtype=jnp.int32)[:, None] // BLOCK == row_ids).astype(BF16)

    def tiles(count):
        return [pltpu.VMEM((nodes, plan.tile), BF16)] * count

    *outs, low, sums, full = call(
        forward_kernel,
        plan,
        [array(rows, hcols)] * n
        + [array(heads, nodes, nodes), array(nodes, hcols, dtype=F32), array(nodes, width)],
        tiles(3) + [pltpu.VMEM((nodes, 2 * HD), BF16)],
        4 * nodes * nodes * HD * heads,
        [*qkv, *xs, key_bias, row_hot],
    )
    pieces = [outs[0]] + [swap(outs[k], "seq", k) for k in range(1, n)]
    attended = jnp.zeros((rows, n * hcols), BF16)
    for k in range(n):
        attended = lax.dynamic_update_slice_in_dim(attended, pieces[k], (z ^ k) * hcols, 1)

    scratch = tiles(4) + [pltpu.VMEM((nodes, nodes), BF16), pltpu.VMEM((nodes, plan.tile), F32)]
    flops = 8 * nodes * nodes * HD * plan.gheads
    common = [*qkv, *grads, low, sums]
    grad_t = []
    if plan.groups > 1:
        grad_other, wgrad_other = call(
            lambda *a: backward_kernel(a[0], True, *a[1:]),
            plan,
            [array(plan.gcols, nodes), array(plan.gcols, width)],
            scratch,
            flops + 2 * nodes * plan.gcols * width,
            [(1 - core).reshape(1), *common, full],
            scalar=True,
        )
        got = swap(wgrad_other, "clus", 1)
        grad_t = [grad_other]
    low = after(low, attended)
    (grad_own,) = call(
        lambda *a: backward_kernel(a[0], False, *a[1:]),
        plan,
        [array(plan.gcols, nodes)],
        scratch,
        flops,
        [core.reshape(1), *qkv, *grads, low, sums],
        scalar=True,
    )
    grad_t = [grad_own, *grad_t]
    half = plan.gcols // 2
    count = 2 * nodes * plan.gcols * width
    if plan.groups > 1:
        lower, upper = call(
            weight_kernel, plan, [array(half, width)] * 2, [], count, [grad_own, full, got]
        )
    else:
        (wgrad,) = call(
            whole_weight_kernel, plan, [array(plan.gcols, width)], [], count, [grad_own, full]
        )
        keep = lax.dynamic_slice_in_dim(wgrad, core * half, half, 0)
        send = lax.dynamic_slice_in_dim(wgrad, (1 - core) * half, half, 0)
        part = add(keep, swap(send, "clus", 1))
        lower, upper = part[: half // 2], part[half // 2 :]
    terms = call(
        term_kernel,
        plan,
        [array(rows, width)] * n,
        [],
        count * plan.groups,
        [core.reshape(1), qkv_weight, *grad_t],
        scalar=True,
    )
    node_grad, begun = reduce_slots(terms, z, n)

    bits = []
    while 2 << len(bits) < m:
        bits.append(2 << len(bits))
    for one, two in zip(bits, bits[::-1]):
        lower, upper = sum_pairs(lower, one), sum_pairs(upper, two)
    part = jnp.concatenate([lower, upper], axis=0)
    got = swap(part, "clus", 1)
    both = jnp.where(core == 0, jnp.stack([part, got]), jnp.stack([got, part]))
    weight_grad = both.reshape(plan.columns, width).astype(F32) / m

    return (attended[None], node_grad[None], weight_grad)


def solution(mesh):
    return jax.shard_map(
        local,
        mesh=mesh,
        in_specs=(
            P("clus", "seq", None),
            P("seq", None),
            P("clus", None, None),
            P("clus", "seq", None),
        ),
        out_specs=(P("clus", "seq", None), P("clus", "seq", None), P("seq", None)),
        check_vma=False,
    )
```

```python
import functools
import math

import jax
import jax.numpy as jnp
from jax import lax
from jax.experimental import pallas as pl
from jax.experimental.pallas import tpu as pltpu
from jax.sharding import PartitionSpec as P

HD = 64
BLOCK = 128
F32 = jnp.float32
BF16 = jnp.bfloat16
NT = (((1,), (1,)), ((), ()))
TN = (((0,), (0,)), ((), ()))
NEVER = -1e30
VMEM = pl.BlockSpec(memory_space=pltpu.VMEM)
SMEM = pl.BlockSpec(memory_space=pltpu.SMEM)


def mm(a, b, dims=(((1,), (0,)), ((), ()))):
    return lax.dot_general(a, b, dims, preferred_element_type=F32)


class Plan:
    def __init__(self, rows, columns, n):
        self.n, self.rows, self.columns = n, rows, columns
        self.nodes = n * rows
        self.heads = columns // (3 * HD)
        self.groups = 2 if self.heads % 2 == 0 else 1
        self.gheads = self.heads // self.groups
        self.pair = self.gheads % 2 == 0
        self.per_tile = 2 if self.pair else 1
        self.tiles = self.gheads // self.per_tile
        self.tile = self.per_tile * HD
        self.gcols = self.gheads * 3 * HD
        self.chunk = BLOCK

    def base(self, group, t):
        start = group * self.gcols + t * 3 * self.tile
        return start if isinstance(start, int) else pl.multiple_of(start, self.tile)

    def feature(self, group, t):
        start = (group * self.tiles + t) * self.tile
        return start if isinstance(start, int) else pl.multiple_of(start, self.tile)


def low_half(shape):
    return lax.broadcasted_iota(jnp.int32, shape, 1) % (2 * HD) < HD


def project_kernel(plan, *refs):
    feats, (weight, full_ref, qkv_ref) = refs[: plan.n - 1], refs[plan.n - 1 :]
    for s, x in enumerate(feats):
        full_ref[s * plan.rows : (s + 1) * plan.rows, :] = x[...]
    qkv_ref[...] = mm(full_ref[...], weight[...], NT).astype(BF16)


def load_tile(plan, qkv, group, t, q_s, k_s, v_s):
    base, tile = plan.base(group, t), plan.tile
    for s in range(plan.n):
        here = slice(s * plan.rows, (s + 1) * plan.rows)
        first, second, third = (qkv[here, pl.ds(base + i * tile, tile)] for i in range(3))
        if plan.pair:
            low = low_half(first.shape)
            queries = jnp.where(low, first, second)
            keys = pltpu.roll(jnp.where(low, third, first).astype(F32), HD, 1).astype(BF16)
            values = jnp.where(low, second, third)
        else:
            queries, keys, values = first, second, third
        q_s[here, :] = (queries.astype(F32) * HD ** -0.5).astype(BF16)
        k_s[here, :] = keys
        v_s[here, :] = values


def with_lanes(plan, h, x, extra):
    if not plan.pair:
        return jnp.concatenate([x, extra[:, :HD]], axis=1)
    low = low_half(x.shape)
    return jnp.where(low if h == 0 else ~low, x, extra)


def only_head(plan, h, x):
    if not plan.pair:
        return x
    low = low_half(x.shape)
    return jnp.where(low if h == 0 else ~low, x, jnp.zeros_like(x))


def merge(plan, h, x, before):
    if not plan.pair or h == 0:
        return x
    return jnp.where(low_half(x.shape), before, x)


def chunks(plan, body):
    steps = plan.nodes // plan.chunk
    if steps <= 4:
        for i in range(steps):
            body(i * plan.chunk)
    else:
        def step(i, carry):
            body(pl.multiple_of(i * plan.chunk, plan.chunk))
            return carry

        lax.fori_loop(0, steps, step, 0)


def forward_kernel(plan, *refs):
    n, rows = plan.n, plan.rows
    known, known_x, last, weight, key_bias, row_hot = refs[:6]
    low_ref, sum_ref, full_ref, qkv = refs[6:10]
    q_s, k_s, v_s, ka_s = refs[10:]
    earlier = (n - 1) * rows
    full_ref[:earlier, :] = known_x[...]
    full_ref[earlier:, :] = last[...]
    qkv[:earlier, :] = known[...]
    qkv[earlier:, :] = mm(last[...], weight[...], NT).astype(BF16)
    for group in range(plan.groups):
        for t in range(plan.tiles):
            load_tile(plan, qkv, group, t, q_s, k_s, v_s)
            lanes = slice(plan.feature(group, t), plan.feature(group, t) + plan.tile)
            for h in range(plan.per_tile):
                head = (group * plan.tiles + t) * plan.per_tile + h
                ka_s[...] = with_lanes(plan, h, k_s[...], key_bias[...])

                def one_chunk(lo):
                    here = pl.ds(lo, plan.chunk)
                    queries = with_lanes(plan, h, q_s[here, :], row_hot[here, :])
                    scores = mm(queries, ka_s[...], NT)
                    unnorm = jnp.exp(scores - jnp.max(scores, axis=-1, keepdims=True))
                    low = (unnorm * (1.0 / jnp.sum(unnorm, axis=-1, keepdims=True))).astype(BF16)
                    low_ref[head, here, :] = low
                    sum_ref[here, lanes] = merge(plan, h, mm(low, v_s[...]), sum_ref[here, lanes])

                chunks(plan, one_chunk)

def backward_kernel(plan, with_weight, *refs):
    n, rows, tile = plan.n, plan.rows, plan.tile
    group = refs[0][0] if plan.groups > 1 else 0
    qkv, grads = refs[1], refs[2 : 2 + n]
    low_ref, sum_ref = refs[2 + n : 4 + n]
    at = 4 + n
    if with_weight:
        full_ref = refs[at]
        at += 1
    grad_ref = refs[at]
    at += 1
    if with_weight:
        wgrad_ref = refs[at]
        at += 1
    q_s, k_s, v_s, g_s, ds_s, dq_s = refs[at:]
    for t in range(plan.tiles):
        load_tile(plan, qkv, group, t, q_s, k_s, v_s)
        feature = plan.feature(group, t)
        for s in range(n):
            g_s[s * rows : (s + 1) * rows, :] = grads[s][:, pl.ds(feature, tile)]
        k_s[...] = (k_s[...].astype(F32) * HD ** -0.5).astype(BF16)
        q_t = q_s[...].T
        g_t = g_s[...].T
        for h in range(plan.per_tile):
            head = (group * plan.tiles + t) * plan.per_tile + h

            def one_chunk(lo):
                here = pl.ds(lo, plan.chunk)
                g_here = only_head(plan, h, g_s[here, :])
                delta = jnp.sum(
                    g_here.astype(F32) * sum_ref[here, pl.ds(feature, tile)], axis=-1, keepdims=True
                )
                grad_weights = mm(g_here, v_s[...], NT)
                ds = (low_ref[head, here, :].astype(F32) * (grad_weights - delta)).astype(BF16)
                ds_s[here, :] = ds
                dq_s[here, :] = merge(plan, h, mm(ds, k_s[...]), dq_s[here, :])

            chunks(plan, one_chunk)
            row = (t * plan.per_tile + h) * 3 * HD
            own = slice(h * HD, (h + 1) * HD)
            grad_ref[row + HD : row + 2 * HD, :] = mm(q_t[own, :], ds_s[...]).astype(BF16)
            grad_ref[row + 2 * HD : row + 3 * HD, :] = mm(g_t[own, :], low_ref[head]).astype(BF16)
        dq_t = dq_s[...].T.astype(BF16)
        for h in range(plan.per_tile):
            row = (t * plan.per_tile + h) * 3 * HD
            grad_ref[row : row + HD, :] = dq_t[h * HD : (h + 1) * HD, :]
    if with_weight:
        wgrad_ref[...] = mm(grad_ref[...], full_ref[...]).astype(BF16)


def weight_kernel(plan, grad_ref, full_ref, got_ref, part_ref):
    part_ref[...] = (mm(grad_ref[...], full_ref[...]) + got_ref[...].astype(F32)).astype(BF16)


def whole_weight_kernel(plan, grad_ref, full_ref, wgrad_ref):
    wgrad_ref[...] = mm(grad_ref[...], full_ref[...]).astype(BF16)


def term_kernel(plan, *refs):
    which, weight, sum_ref = refs[:3]
    grads = refs[3 : 3 + plan.groups]
    sends = refs[3 + plan.groups :]
    width = weight.shape[1]
    for s in reversed(range(plan.n)):
        here = slice(s * plan.rows, (s + 1) * plan.rows)
        total = None
        for i, grad in enumerate(grads):
            if plan.groups > 1:
                group = which[0] if i == 0 else 1 - which[0]
                here_w = pl.ds(pl.multiple_of(group * plan.gcols, plan.gcols), plan.gcols)
            else:
                here_w = slice(None)
            part = mm(grad[:, here], weight[here_w, :], TN)
            total = part if total is None else total + part
        sends[s][:, :width] = total.astype(BF16)
        sends[s][:, width:] = sum_ref[here, :].astype(BF16)


def size(x):
    return math.prod(x.shape) * jnp.dtype(x.dtype).itemsize


def call(kernel, plan, out_shape, scratch, flops, args, scalar=False):
    held = sum(map(size, out_shape)) + sum(map(size, scratch)) + sum(map(size, args))
    held += 32 * plan.chunk * plan.nodes + 24 * plan.nodes * 2 * HD + 8 * 2**20
    return pl.pallas_call(
        functools.partial(kernel, plan),
        out_shape=out_shape,
        in_specs=[SMEM if scalar and i == 0 else VMEM for i in range(len(args))],
        out_specs=[VMEM] * len(out_shape),
        scratch_shapes=scratch,
        compiler_params=pltpu.CompilerParams(vmem_limit_bytes=min(held, 60 * 2**20)),
        cost_estimate=pl.CostEstimate(flops=flops, bytes_accessed=4 << 20, transcendentals=0),
    )(*args)


def array(*shape, dtype=BF16):
    return jax.ShapeDtypeStruct(shape, dtype)


def swap(x, axis, bits):
    size = lax.axis_size(axis)
    return lax.ppermute(x, axis, [(i, i ^ bits) for i in range(size)])


def after(x, *done):
    return lax.optimization_barrier((x, *done))[0]


def add(a, b):
    return (a.astype(F32) + b.astype(F32)).astype(BF16)


def gather_slots(x, z, n):
    if n != 4:
        return [x] + [swap(x, "seq", k) for k in range(1, n)]
    far = swap(x, "seq", 2)
    near = swap(x, "seq", 1)
    ends = lax.ppermute(far, "seq", [(2, 3), (1, 0)])
    middle = lax.ppermute(after(x, far), "seq", [(1, 2), (2, 1)])
    inner = (z == 1) | (z == 2)
    return [x, near, far, jnp.where(inner, middle, ends)]


def local(node_feats, qkv_weight, block_pairs, grad_out):
    feats = node_feats[0]
    rows, width = feats.shape
    n, m = lax.axis_size("seq"), lax.axis_size("clus")
    z, c = lax.axis_index("seq"), lax.axis_index("clus")
    plan = Plan(rows, qkv_weight.shape[0], n)
    nodes, heads = plan.nodes, plan.heads
    core = c % 2

    xs = gather_slots(feats, z, n)
    hcols = heads * HD

    def for_slot(k):
        return lax.dynamic_slice_in_dim(grad_out[0], (z ^ k) * hcols, hcols, 1)

    own, *sent = after([for_slot(k) for k in range(n)], *xs[1:3])
    grads = [own] + [swap(sent[k - 1], "seq", k) for k in range(1, n)]

    earlier = nodes - rows
    known_x, known = call(
        project_kernel,
        plan,
        [array(earlier, width), array(earlier, plan.columns)],
        [],
        2 * earlier * plan.columns * width,
        [*xs[:-1], qkv_weight],
    )

    per_dev = rows // BLOCK
    blocks = nodes // BLOCK
    listed = block_pairs[0]
    place = ((listed // per_dev) ^ z) * per_dev + listed % per_dev
    ids = jnp.arange(blocks, dtype=jnp.int32)
    row_ids = jnp.arange(2 * HD, dtype=jnp.int32) % HD
    allowed = jnp.any(
        (place[:, 0, None, None] == row_ids) & (place[:, 1, None, None] == ids[:, None]), axis=0
    )
    blocked = ~allowed & (row_ids < blocks)
    key_bias = jnp.repeat(jnp.where(blocked, NEVER, 0.0).astype(BF16), BLOCK, axis=0)
    row_hot = (jnp.arange(nodes, dtype=jnp.int32)[:, None] // BLOCK == row_ids).astype(BF16)

    def tiles(count):
        return [pltpu.VMEM((nodes, plan.tile), BF16)] * count

    low, sums, full, qkv = call(
        forward_kernel,
        plan,
        [array(heads, nodes, nodes), array(nodes, hcols, dtype=F32), array(nodes, width), array(nodes, plan.columns)],
        tiles(3) + [pltpu.VMEM((nodes, 2 * HD), BF16)],
        4 * nodes * nodes * HD * heads,
        [known, known_x, xs[-1], qkv_weight, key_bias, row_hot],
    )
    scratch = tiles(4) + [pltpu.VMEM((nodes, nodes), BF16), pltpu.VMEM((nodes, plan.tile), F32)]
    flops = 8 * nodes * nodes * HD * plan.gheads
    common = [qkv, *grads, low, sums]
    grad_t = []
    if plan.groups > 1:
        grad_other, wgrad_other = call(
            lambda *a: backward_kernel(a[0], True, *a[1:]),
            plan,
            [array(plan.gcols, nodes), array(plan.gcols, width)],
            scratch,
            flops + 2 * nodes * plan.gcols * width,
            [(1 - core).reshape(1), *common, full],
            scalar=True,
        )
        got = swap(wgrad_other, "clus", 1)
        grad_t = [grad_other]
    (grad_own,) = call(
        lambda *a: backward_kernel(a[0], False, *a[1:]),
        plan,
        [array(plan.gcols, nodes)],
        scratch,
        flops,
        [core.reshape(1), qkv, *grads, low, sums],
        scalar=True,
    )
    grad_t = [grad_own, *grad_t]
    count = 2 * nodes * plan.gcols * width
    if plan.groups > 1:
        (part,) = call(
            weight_kernel, plan, [array(plan.gcols, width)], [], count, [grad_own, full, got]
        )
    else:
        half = plan.gcols // 2
        (wgrad,) = call(
            whole_weight_kernel, plan, [array(plan.gcols, width)], [], count, [grad_own, full]
        )
        keep = lax.dynamic_slice_in_dim(wgrad, core * half, half, 0)
        send = lax.dynamic_slice_in_dim(wgrad, (1 - core) * half, half, 0)
        part = add(keep, swap(send, "clus", 1))
    sends = call(
        term_kernel,
        plan,
        [array(rows, width + hcols)] * n,
        [],
        count * plan.groups,
        [core.reshape(1), qkv_weight, sums, *grad_t],
        scalar=True,
    )
    received = [sends[0]] + [swap(sends[k], "seq", k) for k in range(1, n)]

    bits = []
    while 2 << len(bits) < m:
        bits.append(2 << len(bits))

    def across(x, stage):
        pairs = [(i, i ^ (bits[-1 - stage] if i % 2 else bits[stage])) for i in range(m)]
        return lax.ppermute(x, "clus", pairs)

    def finish(part, got):
        part = add(part, got)
        for stage in range(1, len(bits)):
            part = add(part, across(part, stage))
        got = swap(part, "clus", 1)
        both = jnp.where(core == 0, jnp.stack([part, got]), jnp.stack([got, part]))
        return both.reshape(plan.columns, width).astype(F32) / m

    got = across(part, 0)
    weight_grad = lax.cond(
        listed[0, 0] >= 0,
        finish,
        lambda part, got: jnp.zeros((plan.columns, width), F32),
        part,
        got,
    )

    received = after(received, weight_grad)
    node_grad = sum(x[:, :width].astype(F32) for x in received).astype(BF16)
    attended = jnp.zeros((rows, n * hcols), BF16)
    for k in range(n):
        attended = lax.dynamic_update_slice_in_dim(attended, received[k][:, width:], (z ^ k) * hcols, 1)
    return (attended[None], node_grad[None], weight_grad)


def solution(mesh):
    return jax.shard_map(
        local,
        mesh=mesh,
        in_specs=(
            P("clus", "seq", None),
            P("seq", None),
            P("clus", None, None),
            P("clus", "seq", None),
        ),
        out_specs=(P("clus", "seq", None), P("clus", "seq", None), P("seq", None)),
        check_vma=False,
    )
```

```python
import functools
import math

import jax
import jax.numpy as jnp
from jax import lax
from jax.experimental import pallas as pl
from jax.experimental.pallas import tpu as pltpu
from jax.sharding import PartitionSpec as P

HD = 64
BLOCK = 128
F32 = jnp.float32
BF16 = jnp.bfloat16
NT = (((1,), (1,)), ((), ()))
TN = (((0,), (0,)), ((), ()))
NEVER = -1e30
VMEM = pl.BlockSpec(memory_space=pltpu.VMEM)
SMEM = pl.BlockSpec(memory_space=pltpu.SMEM)


def mm(a, b, dims=(((1,), (0,)), ((), ()))):
    return lax.dot_general(a, b, dims, preferred_element_type=F32)


class Plan:
    def __init__(self, rows, columns, n):
        self.n, self.rows, self.columns = n, rows, columns
        self.nodes = n * rows
        self.heads = columns // (3 * HD)
        self.groups = 2 if self.heads % 2 == 0 else 1
        self.gheads = self.heads // self.groups
        self.pair = self.gheads % 2 == 0
        self.per_tile = 2 if self.pair else 1
        self.tiles = self.gheads // self.per_tile
        self.tile = self.per_tile * HD
        self.gcols = self.gheads * 3 * HD
        self.chunk = BLOCK

    def base(self, group, t):
        start = group * self.gcols + t * 3 * self.tile
        return start if isinstance(start, int) else pl.multiple_of(start, self.tile)

    def feature(self, group, t):
        start = (group * self.tiles + t) * self.tile
        return start if isinstance(start, int) else pl.multiple_of(start, self.tile)


def low_half(shape):
    return lax.broadcasted_iota(jnp.int32, shape, 1) % (2 * HD) < HD


def project_kernel(plan, *refs):
    feats, (weight, full_ref, qkv_ref) = refs[: plan.n - 1], refs[plan.n - 1 :]
    for s, x in enumerate(feats):
        full_ref[s * plan.rows : (s + 1) * plan.rows, :] = x[...]
    qkv_ref[...] = mm(full_ref[...], weight[...], NT).astype(BF16)


def load_tile(plan, qkv, group, t, q_s, k_s, v_s):
    base, tile = plan.base(group, t), plan.tile
    for s in range(plan.n):
        here = slice(s * plan.rows, (s + 1) * plan.rows)
        first, second, third = (qkv[here, pl.ds(base + i * tile, tile)] for i in range(3))
        if plan.pair:
            low = low_half(first.shape)
            queries = jnp.where(low, first, second)
            keys = pltpu.roll(jnp.where(low, third, first).astype(F32), HD, 1).astype(BF16)
            values = jnp.where(low, second, third)
        else:
            queries, keys, values = first, second, third
        q_s[here, :] = (queries.astype(F32) * HD ** -0.5).astype(BF16)
        k_s[here, :] = keys
        v_s[here, :] = values


def with_lanes(plan, h, x, extra):
    if not plan.pair:
        return jnp.concatenate([x, extra[:, :HD]], axis=1)
    low = low_half(x.shape)
    return jnp.where(low if h == 0 else ~low, x, extra)


def only_head(plan, h, x):
    if not plan.pair:
        return x
    low = low_half(x.shape)
    return jnp.where(low if h == 0 else ~low, x, jnp.zeros_like(x))


def merge(plan, h, x, before):
    if not plan.pair or h == 0:
        return x
    return jnp.where(low_half(x.shape), before, x)


def chunks(plan, body):
    steps = plan.nodes // plan.chunk
    if steps <= 4:
        for i in range(steps):
            body(i * plan.chunk)
    else:
        def step(i, carry):
            body(pl.multiple_of(i * plan.chunk, plan.chunk))
            return carry

        lax.fori_loop(0, steps, step, 0)


def forward_kernel(plan, *refs):
    n, rows = plan.n, plan.rows
    known, known_x, last, weight, key_bias, row_hot = refs[:6]
    low_ref, sum_ref, full_ref, qkv = refs[6:10]
    q_s, k_s, v_s, ka_s = refs[10:]
    earlier = (n - 1) * rows
    full_ref[:earlier, :] = known_x[...]
    full_ref[earlier:, :] = last[...]
    qkv[:earlier, :] = known[...]
    qkv[earlier:, :] = mm(last[...], weight[...], NT).astype(BF16)
    for group in range(plan.groups):
        for t in range(plan.tiles):
            load_tile(plan, qkv, group, t, q_s, k_s, v_s)
            lanes = slice(plan.feature(group, t), plan.feature(group, t) + plan.tile)
            for h in range(plan.per_tile):
                head = (group * plan.tiles + t) * plan.per_tile + h
                ka_s[...] = with_lanes(plan, h, k_s[...], key_bias[...])

                def one_chunk(lo):
                    here = pl.ds(lo, plan.chunk)
                    queries = with_lanes(plan, h, q_s[here, :], row_hot[here, :])
                    scores = mm(queries, ka_s[...], NT)
                    unnorm = jnp.exp(scores - jnp.max(scores, axis=-1, keepdims=True))
                    low = (unnorm * (1.0 / jnp.sum(unnorm, axis=-1, keepdims=True))).astype(BF16)
                    low_ref[head, here, :] = low
                    sum_ref[here, lanes] = merge(plan, h, mm(low, v_s[...]), sum_ref[here, lanes])

                chunks(plan, one_chunk)

def backward_kernel(plan, with_weight, *refs):
    n, rows, tile = plan.n, plan.rows, plan.tile
    group = refs[0][0] if plan.groups > 1 else 0
    qkv, grads = refs[1], refs[2 : 2 + n]
    low_ref, sum_ref = refs[2 + n : 4 + n]
    at = 4 + n
    if with_weight:
        full_ref = refs[at]
        at += 1
    grad_ref = refs[at]
    at += 1
    if with_weight:
        wgrad_ref = refs[at]
        at += 1
    q_s, k_s, v_s, g_s, ds_s, dq_s = refs[at:]
    for t in range(plan.tiles):
        load_tile(plan, qkv, group, t, q_s, k_s, v_s)
        feature = plan.feature(group, t)
        for s in range(n):
            g_s[s * rows : (s + 1) * rows, :] = grads[s][:, pl.ds(feature, tile)]
        k_s[...] = (k_s[...].astype(F32) * HD ** -0.5).astype(BF16)
        q_t = q_s[...].T
        g_t = g_s[...].T
        for h in range(plan.per_tile):
            head = (group * plan.tiles + t) * plan.per_tile + h

            def one_chunk(lo):
                here = pl.ds(lo, plan.chunk)
                g_here = only_head(plan, h, g_s[here, :])
                delta = jnp.sum(
                    g_here.astype(F32) * sum_ref[here, pl.ds(feature, tile)], axis=-1, keepdims=True
                )
                grad_weights = mm(g_here, v_s[...], NT)
                ds = (low_ref[head, here, :].astype(F32) * (grad_weights - delta)).astype(BF16)
                ds_s[here, :] = ds
                dq_s[here, :] = merge(plan, h, mm(ds, k_s[...]), dq_s[here, :])

            chunks(plan, one_chunk)
            row = (t * plan.per_tile + h) * 3 * HD
            own = slice(h * HD, (h + 1) * HD)
            grad_ref[row + HD : row + 2 * HD, :] = mm(q_t[own, :], ds_s[...]).astype(BF16)
            grad_ref[row + 2 * HD : row + 3 * HD, :] = mm(g_t[own, :], low_ref[head]).astype(BF16)
        dq_t = dq_s[...].T.astype(BF16)
        for h in range(plan.per_tile):
            row = (t * plan.per_tile + h) * 3 * HD
            grad_ref[row : row + HD, :] = dq_t[h * HD : (h + 1) * HD, :]
    if with_weight:
        wgrad_ref[...] = mm(grad_ref[...], full_ref[...]).astype(BF16)


def weight_kernel(plan, grad_ref, full_ref, got_ref, *parts):
    size = parts[0].shape[0]
    for i, part in enumerate(parts):
        here = slice(i * size, (i + 1) * size)
        product = mm(grad_ref[here, :], full_ref[...])
        part[...] = (product + got_ref[here, :].astype(F32)).astype(BF16)


def whole_weight_kernel(plan, grad_ref, full_ref, wgrad_ref):
    wgrad_ref[...] = mm(grad_ref[...], full_ref[...]).astype(BF16)


def term_kernel(plan, *refs):
    which, weight, sum_ref = refs[:3]
    grads = refs[3 : 3 + plan.groups]
    sends = refs[3 + plan.groups :]
    width = weight.shape[1]
    for s in reversed(range(plan.n)):
        here = slice(s * plan.rows, (s + 1) * plan.rows)
        total = None
        for i, grad in enumerate(grads):
            if plan.groups > 1:
                group = which[0] if i == 0 else 1 - which[0]
                here_w = pl.ds(pl.multiple_of(group * plan.gcols, plan.gcols), plan.gcols)
            else:
                here_w = slice(None)
            part = mm(grad[:, here], weight[here_w, :], TN)
            total = part if total is None else total + part
        sends[s][:, :width] = total.astype(BF16)
        sends[s][:, width:] = sum_ref[here, :].astype(BF16)


def scale_kernel(plan, m, which, *refs):
    out = refs[-1]
    count = (len(refs) - 1) // 2
    size = refs[0].shape[0]
    for i, ref in enumerate(refs[:-1]):
        side = which[0] if i < count else 1 - which[0]
        start = side * (count * size) + (i % count) * size
        out[pl.ds(pl.multiple_of(start, size), size), :] = ref[...].astype(F32) * (1.0 / m)


def combine_kernel(plan, place, *refs):
    n, hcols = plan.n, plan.heads * HD
    received, (node_grad, attended) = refs[:-2], refs[-2:]
    width = node_grad.shape[1]
    pieces = [x[:, width : width + hcols] for x in received[:n]]
    terms = [x[:, :width] for x in received[:n]]
    total = terms[0].astype(F32)
    for term in terms[1:]:
        total = total + term.astype(F32)
    node_grad[...] = total.astype(BF16)
    for k, piece in enumerate(pieces):
        start = (place[0] ^ k) * hcols
        if hcols % 128 == 0:
            attended[:, pl.ds(pl.multiple_of(start, hcols), hcols)] = piece
        else:
            attended[k, :, :] = piece


def size(x):
    return math.prod(x.shape) * jnp.dtype(x.dtype).itemsize


def call(kernel, plan, out_shape, scratch, flops, args, scalar=False):
    held = sum(map(size, out_shape)) + sum(map(size, scratch)) + sum(map(size, args))
    held += 32 * plan.chunk * plan.nodes + 24 * plan.nodes * 2 * HD + 8 * 2**20
    return pl.pallas_call(
        functools.partial(kernel, plan),
        out_shape=out_shape,
        in_specs=[SMEM if scalar and i == 0 else VMEM for i in range(len(args))],
        out_specs=[VMEM] * len(out_shape),
        scratch_shapes=scratch,
        compiler_params=pltpu.CompilerParams(vmem_limit_bytes=min(held, 60 * 2**20)),
        cost_estimate=pl.CostEstimate(flops=flops, bytes_accessed=4 << 20, transcendentals=0),
    )(*args)


def array(*shape, dtype=BF16):
    return jax.ShapeDtypeStruct(shape, dtype)


def swap(x, axis, bits):
    size = lax.axis_size(axis)
    return lax.ppermute(x, axis, [(i, i ^ bits) for i in range(size)])


def after(x, *done):
    return lax.optimization_barrier((x, *done))[0]


def add(a, b):
    return (a.astype(F32) + b.astype(F32)).astype(BF16)


def exchange_slots(plan, sends, n):
    return [sends[0]] + [swap(sends[k], "seq", k) for k in range(1, n)]


def gather_slots(x, z, n):
    if n != 4:
        return [x] + [swap(x, "seq", k) for k in range(1, n)]
    far = swap(x, "seq", 2)
    near = swap(x, "seq", 1)
    ends = lax.ppermute(far, "seq", [(2, 3), (1, 0)])
    middle = lax.ppermute(after(x, far), "seq", [(1, 2), (2, 1)])
    inner = (z == 1) | (z == 2)
    return [x, near, far, jnp.where(inner, middle, ends)]


def local(node_feats, qkv_weight, block_pairs, grad_out):
    feats = node_feats[0]
    rows, width = feats.shape
    n, m = lax.axis_size("seq"), lax.axis_size("clus")
    z, c = lax.axis_index("seq"), lax.axis_index("clus")
    plan = Plan(rows, qkv_weight.shape[0], n)
    nodes, heads = plan.nodes, plan.heads
    core = c % 2

    xs = gather_slots(feats, z, n)
    hcols = heads * HD

    def for_slot(k):
        return lax.dynamic_slice_in_dim(grad_out[0], (z ^ k) * hcols, hcols, 1)

    earlier = nodes - rows
    known_x, known = call(
        project_kernel,
        plan,
        [array(earlier, width), array(earlier, plan.columns)],
        [],
        2 * earlier * plan.columns * width,
        [*xs[:-1], qkv_weight],
    )

    own, *sent = after([for_slot(k) for k in range(n)], known)
    grads = [own] + [swap(sent[k - 1], "seq", k) for k in range(1, n)]

    per_dev = rows // BLOCK
    blocks = nodes // BLOCK
    listed = block_pairs[0]
    place = ((listed // per_dev) ^ z) * per_dev + listed % per_dev
    ids = jnp.arange(blocks, dtype=jnp.int32)
    row_ids = jnp.arange(2 * HD, dtype=jnp.int32) % HD
    allowed = jnp.any(
        (place[:, 0, None, None] == row_ids) & (place[:, 1, None, None] == ids[:, None]), axis=0
    )
    blocked = ~allowed & (row_ids < blocks)
    key_bias = jnp.repeat(jnp.where(blocked, NEVER, 0.0).astype(BF16), BLOCK, axis=0)
    row_hot = (jnp.arange(nodes, dtype=jnp.int32)[:, None] // BLOCK == row_ids).astype(BF16)

    def tiles(count):
        return [pltpu.VMEM((nodes, plan.tile), BF16)] * count

    low, sums, full, qkv = call(
        forward_kernel,
        plan,
        [array(heads, nodes, nodes), array(nodes, hcols, dtype=F32), array(nodes, width), array(nodes, plan.columns)],
        tiles(3) + [pltpu.VMEM((nodes, 2 * HD), BF16)],
        4 * nodes * nodes * HD * heads,
        [known, known_x, xs[-1], qkv_weight, key_bias, row_hot],
    )
    scratch = tiles(4) + [pltpu.VMEM((nodes, nodes), BF16), pltpu.VMEM((nodes, plan.tile), F32)]
    flops = 8 * nodes * nodes * HD * plan.gheads
    common = [qkv, *grads, low, sums]
    grad_t = []
    if plan.groups > 1:
        grad_other, wgrad_other = call(
            lambda *a: backward_kernel(a[0], True, *a[1:]),
            plan,
            [array(plan.gcols, nodes), array(plan.gcols, width)],
            scratch,
            flops + 2 * nodes * plan.gcols * width,
            [(1 - core).reshape(1), *common, full],
            scalar=True,
        )
        got = swap(wgrad_other, "clus", 1)
        grad_t = [grad_other]
    (grad_own,) = call(
        lambda *a: backward_kernel(a[0], False, *a[1:]),
        plan,
        [array(plan.gcols, nodes)],
        scratch,
        flops,
        [core.reshape(1), qkv, *grads, low, sums],
        scalar=True,
    )
    grad_t = [grad_own, *grad_t]
    count = 2 * nodes * plan.gcols * width
    half = plan.gcols // 2
    if plan.groups > 1:
        parts = call(
            weight_kernel, plan, [array(half, width)] * 2, [], count, [grad_own, full, got]
        )
    else:
        (wgrad,) = call(
            whole_weight_kernel, plan, [array(plan.gcols, width)], [], count, [grad_own, full]
        )
        keep = lax.dynamic_slice_in_dim(wgrad, core * half, half, 0)
        send = lax.dynamic_slice_in_dim(wgrad, (1 - core) * half, half, 0)
        parts = [add(keep, swap(send, "clus", 1))]
    sends = call(
        term_kernel,
        plan,
        [array(rows, width + hcols)] * n,
        [],
        count * plan.groups,
        [core.reshape(1), qkv_weight, sums, *grad_t],
        scalar=True,
    )
    received = exchange_slots(plan, sends, n)

    bits = []
    while 2 << len(bits) < m:
        bits.append(2 << len(bits))

    def across(x, stage):
        pairs = [(i, i ^ (bits[-1 - stage] if i % 2 else bits[stage])) for i in range(m)]
        return lax.ppermute(x, "clus", pairs)

    def finish(parts, gots):
        parts = [add(part, got) for part, got in zip(parts, gots)]
        for stage in range(1, len(bits)):
            gots = [across(part, stage) for part in parts]
            parts = [add(part, got) for part, got in zip(parts, gots)]
        gots = [swap(part, "clus", 1) for part in parts]
        (result,) = call(
            lambda *a: scale_kernel(a[0], m, *a[1:]),
            plan,
            [array(plan.columns, width, dtype=F32)],
            [],
            0,
            [core.reshape(1), *parts, *gots],
            scalar=True,
        )
        return result

    gots = [across(part, 0) for part in parts]
    weight_grad = lax.cond(
        listed[0, 0] >= 0,
        finish,
        lambda parts, gots: jnp.zeros((plan.columns, width), F32),
        parts,
        gots,
    )

    received = after(received, weight_grad)
    aligned = hcols % 128 == 0
    node_grad, attended = call(
        combine_kernel,
        plan,
        [array(rows, width), array(rows, n * hcols) if aligned else array(n, rows, hcols)],
        [],
        0,
        [z.reshape(1), *received],
        scalar=True,
    )
    if not aligned:
        order = jnp.arange(n, dtype=jnp.int32) ^ z
        attended = attended[order].transpose(1, 0, 2).reshape(rows, n * hcols)
    return (attended[None], node_grad[None], weight_grad)


def solution(mesh):
    return jax.shard_map(
        local,
        mesh=mesh,
        in_specs=(
            P("clus", "seq", None),
            P("seq", None),
            P("clus", None, None),
            P("clus", "seq", None),
        ),
        out_specs=(P("clus", "seq", None), P("clus", "seq", None), P("seq", None)),
        check_vma=False,
    )
```

```python
import functools
import math

import jax
import jax.numpy as jnp
from jax import lax
from jax.experimental import pallas as pl
from jax.experimental.pallas import tpu as pltpu
from jax.sharding import PartitionSpec as P

HD = 64
BLOCK = 128
F32 = jnp.float32
BF16 = jnp.bfloat16
NT = (((1,), (1,)), ((), ()))
TN = (((0,), (0,)), ((), ()))
NEVER = -1e30
VMEM = pl.BlockSpec(memory_space=pltpu.VMEM)
HBM = pl.BlockSpec(memory_space=pltpu.HBM)
SMEM = pl.BlockSpec(memory_space=pltpu.SMEM)


def mm(a, b, dims=(((1,), (0,)), ((), ()))):
    return lax.dot_general(a, b, dims, preferred_element_type=F32)


class Plan:
    def __init__(self, rows, columns, n):
        self.n, self.rows, self.columns = n, rows, columns
        self.nodes = n * rows
        self.heads = columns // (3 * HD)
        self.groups = 2 if self.heads % 2 == 0 else 1
        self.gheads = self.heads // self.groups
        self.pair = self.gheads % 2 == 0
        self.per_tile = 2 if self.pair else 1
        self.tiles = self.gheads // self.per_tile
        self.tile = self.per_tile * HD
        self.gcols = self.gheads * 3 * HD
        self.chunk = math.gcd(self.nodes, 512)

    def base(self, group, t):
        start = group * self.gcols + t * 3 * self.tile
        return start if isinstance(start, int) else pl.multiple_of(start, self.tile)

    def feature(self, group, t):
        start = (group * self.tiles + t) * self.tile
        return start if isinstance(start, int) else pl.multiple_of(start, self.tile)


def low_half(shape):
    return lax.broadcasted_iota(jnp.int32, shape, 1) % (2 * HD) < HD


def project_kernel(plan, *refs):
    feats, (weight, full_ref, qkv_ref) = refs[: plan.n - 1], refs[plan.n - 1 :]
    for s, x in enumerate(feats):
        full_ref[s * plan.rows : (s + 1) * plan.rows, :] = x[...]
    qkv_ref[...] = mm(full_ref[...], weight[...], NT).astype(BF16)


def load_tile(plan, qkv, group, t, q_s, k_s, v_s):
    base, tile = plan.base(group, t), plan.tile
    for s in range(plan.n):
        here = slice(s * plan.rows, (s + 1) * plan.rows)
        first, second, third = (qkv[here, pl.ds(base + i * tile, tile)] for i in range(3))
        if plan.pair:
            low = low_half(first.shape)
            queries = jnp.where(low, first, second)
            keys = pltpu.roll(jnp.where(low, third, first).astype(F32), HD, 1).astype(BF16)
            values = jnp.where(low, second, third)
        else:
            queries, keys, values = first, second, third
        q_s[here, :] = (queries.astype(F32) * HD ** -0.5).astype(BF16)
        k_s[here, :] = keys
        v_s[here, :] = values


def with_lanes(plan, h, x, extra):
    if not plan.pair:
        return jnp.concatenate([x, extra[:, :HD]], axis=1)
    low = low_half(x.shape)
    return jnp.where(low if h == 0 else ~low, x, extra)


def only_head(plan, h, x):
    if not plan.pair:
        return x
    low = low_half(x.shape)
    return jnp.where(low if h == 0 else ~low, x, jnp.zeros_like(x))


def merge(plan, h, x, before):
    if not plan.pair or h == 0:
        return x
    return jnp.where(low_half(x.shape), before, x)


def chunks(plan, body):
    steps = plan.nodes // plan.chunk
    if steps <= 4:
        for i in range(steps):
            body(i * plan.chunk)
    else:
        def step(i, carry):
            body(pl.multiple_of(i * plan.chunk, plan.chunk))
            return carry

        lax.fori_loop(0, steps, step, 0)


def forward_kernel(plan, *refs):
    n, rows = plan.n, plan.rows
    known, known_x, last, weight, key_bias, row_hot = refs[:6]
    low_ref, sum_ref, full_ref, qkv = refs[6:10]
    q_s, k_s, v_s, ka_s = refs[10:]
    earlier = (n - 1) * rows
    full_ref[:earlier, :] = known_x[...]
    full_ref[earlier:, :] = last[...]
    qkv[:earlier, :] = known[...]
    qkv[earlier:, :] = mm(last[...], weight[...], NT).astype(BF16)
    for group in range(plan.groups):
        for t in range(plan.tiles):
            load_tile(plan, qkv, group, t, q_s, k_s, v_s)
            lanes = slice(plan.feature(group, t), plan.feature(group, t) + plan.tile)
            for h in range(plan.per_tile):
                head = (group * plan.tiles + t) * plan.per_tile + h
                ka_s[...] = with_lanes(plan, h, k_s[...], key_bias[...])

                def one_chunk(lo):
                    here = pl.ds(lo, plan.chunk)
                    queries = with_lanes(plan, h, q_s[here, :], row_hot[here, :])
                    scores = mm(queries, ka_s[...], NT)
                    unnorm = jnp.exp(scores - jnp.max(scores, axis=-1, keepdims=True))
                    low = (unnorm * (1.0 / jnp.sum(unnorm, axis=-1, keepdims=True))).astype(BF16)
                    low_ref[head, here, :] = low
                    sum_ref[here, lanes] = merge(plan, h, mm(low, v_s[...]), sum_ref[here, lanes])

                chunks(plan, one_chunk)

def backward_kernel(plan, with_weight, *refs):
    n, rows, tile = plan.n, plan.rows, plan.tile
    group = refs[0][0] if plan.groups > 1 else 0
    qkv, grads = refs[1], refs[2 : 2 + n]
    low_ref, sum_ref = refs[2 + n : 4 + n]
    at = 4 + n
    if with_weight:
        full_ref = refs[at]
        at += 1
    grad_ref = refs[at]
    at += 1
    if with_weight:
        wgrad_ref = refs[at]
        at += 1
    q_s, k_s, v_s, g_s, ds_s, dq_s = refs[at:]
    for t in range(plan.tiles):
        load_tile(plan, qkv, group, t, q_s, k_s, v_s)
        feature = plan.feature(group, t)
        for s in range(n):
            g_s[s * rows : (s + 1) * rows, :] = grads[s][:, pl.ds(feature, tile)]
        k_s[...] = (k_s[...].astype(F32) * HD ** -0.5).astype(BF16)
        q_t = q_s[...].T
        g_t = g_s[...].T
        for h in range(plan.per_tile):
            head = (group * plan.tiles + t) * plan.per_tile + h

            def one_chunk(lo):
                here = pl.ds(lo, plan.chunk)
                g_here = only_head(plan, h, g_s[here, :])
                delta = jnp.sum(
                    g_here.astype(F32) * sum_ref[here, pl.ds(feature, tile)], axis=-1, keepdims=True
                )
                grad_weights = mm(g_here, v_s[...], NT)
                ds = (low_ref[head, here, :].astype(F32) * (grad_weights - delta)).astype(BF16)
                ds_s[here, :] = ds
                dq_s[here, :] = merge(plan, h, mm(ds, k_s[...]), dq_s[here, :])

            chunks(plan, one_chunk)
            row = (t * plan.per_tile + h) * 3 * HD
            own = slice(h * HD, (h + 1) * HD)
            grad_ref[row + HD : row + 2 * HD, :] = mm(q_t[own, :], ds_s[...]).astype(BF16)
            grad_ref[row + 2 * HD : row + 3 * HD, :] = mm(g_t[own, :], low_ref[head]).astype(BF16)
        dq_t = dq_s[...].T.astype(BF16)
        for h in range(plan.per_tile):
            row = (t * plan.per_tile + h) * 3 * HD
            grad_ref[row : row + HD, :] = dq_t[h * HD : (h + 1) * HD, :]
    if with_weight:
        wgrad_ref[...] = mm(grad_ref[...], full_ref[...]).astype(BF16)


def weight_kernel(plan, grad_ref, full_ref, got_ref, *parts):
    size = parts[0].shape[0]
    for i, part in enumerate(parts):
        here = slice(i * size, (i + 1) * size)
        product = mm(grad_ref[here, :], full_ref[...])
        part[...] = (product + got_ref[here, :].astype(F32)).astype(BF16)


def whole_weight_kernel(plan, grad_ref, full_ref, wgrad_ref):
    wgrad_ref[...] = mm(grad_ref[...], full_ref[...]).astype(BF16)


def term_kernel(plan, *refs):
    which, weight, sum_ref = refs[:3]
    grads = refs[3 : 3 + plan.groups]
    sends = refs[3 + plan.groups :]
    width = weight.shape[1]
    for s in reversed(range(plan.n)):
        here = slice(s * plan.rows, (s + 1) * plan.rows)
        total = None
        for i, grad in enumerate(grads):
            if plan.groups > 1:
                group = which[0] if i == 0 else 1 - which[0]
                here_w = pl.ds(pl.multiple_of(group * plan.gcols, plan.gcols), plan.gcols)
            else:
                here_w = slice(None)
            part = mm(grad[:, here], weight[here_w, :], TN)
            total = part if total is None else total + part
        sends[s][:, :width] = total.astype(BF16)
        sends[s][:, width:] = sum_ref[here, :].astype(BF16)


def scale_kernel(plan, m, places, which, *refs):
    out, staged, sems = refs[-3:]
    parts = refs[-3 - len(places) : -3]
    size = parts[0].shape[0]
    copies = []
    for i, (own, index, count) in enumerate(places):
        side = which[0] if own else 1 - which[0]
        start = pl.multiple_of((side * count + index) * size, size)
        staged[i] = parts[i][...].astype(F32) * (1.0 / m)
        copies.append(pltpu.make_async_copy(staged.at[i], out.at[pl.ds(start, size), :], sems.at[i]))
        copies[-1].start()
    for copy in copies:
        copy.wait()


def scaled(plan, m, core, parts, places, whole=None):
    rows, width = parts[0].shape
    count = len(parts)
    args = [core.reshape(1), *([] if whole is None else [whole]), *parts]
    specs = [SMEM] + [HBM] * (whole is not None) + [VMEM] * count
    return pl.pallas_call(
        functools.partial(scale_kernel, plan, m, places),
        out_shape=array(2 * places[0][2] * rows, width, dtype=F32),
        in_specs=specs,
        out_specs=HBM,
        scratch_shapes=[pltpu.VMEM((count, rows, width), F32), pltpu.SemaphoreType.DMA((count,))],
        input_output_aliases={} if whole is None else {1: 0},
        compiler_params=pltpu.CompilerParams(vmem_limit_bytes=12 * 2**20),
        cost_estimate=pl.CostEstimate(flops=0, bytes_accessed=1 << 20, transcendentals=0),
    )(*args)


def relay_kernel(plan, own, ahead, out):
    wide = own.shape[1]
    width = wide - plan.heads * HD
    out[:, :width] = add(own[:, :width], ahead[:, :width])
    out[:, width:wide] = own[:, width:]
    out[:, wide:] = ahead[:, width:]


def combine_kernel(plan, place, *refs):
    hcols = plan.heads * HD
    received, (node_grad, attended) = refs[:-2], refs[-2:]
    width = node_grad.shape[1]
    total = received[0][:, :width].astype(F32)
    for x in received[1:]:
        total = total + x[:, :width].astype(F32)
    node_grad[...] = total.astype(BF16)
    slot = 0
    for x in received:
        for at in range(width, x.shape[1], hcols):
            if hcols % 128 == 0:
                start = pl.multiple_of((place[0] ^ slot) * hcols, hcols)
                attended[:, pl.ds(start, hcols)] = x[:, at : at + hcols]
            else:
                attended[slot, :, :] = x[:, at : at + hcols]
            slot += 1


def size(x):
    return math.prod(x.shape) * jnp.dtype(x.dtype).itemsize


def call(kernel, plan, out_shape, scratch, flops, args, scalar=False):
    held = sum(map(size, out_shape)) + sum(map(size, scratch)) + sum(map(size, args))
    held += 32 * plan.chunk * plan.nodes + 24 * plan.nodes * 2 * HD + 8 * 2**20
    return pl.pallas_call(
        functools.partial(kernel, plan),
        out_shape=out_shape,
        in_specs=[SMEM if scalar and i == 0 else VMEM for i in range(len(args))],
        out_specs=[VMEM] * len(out_shape),
        scratch_shapes=scratch,
        compiler_params=pltpu.CompilerParams(vmem_limit_bytes=min(held, 60 * 2**20)),
        cost_estimate=pl.CostEstimate(flops=flops, bytes_accessed=4 << 20, transcendentals=0),
    )(*args)


def array(*shape, dtype=BF16):
    return jax.ShapeDtypeStruct(shape, dtype)


def swap(x, axis, bits):
    size = lax.axis_size(axis)
    return lax.ppermute(x, axis, [(i, i ^ bits) for i in range(size)])


def after(x, *done):
    return lax.optimization_barrier((x, *done))[0]


def add(a, b):
    return (a.astype(F32) + b.astype(F32)).astype(BF16)


def gather_slots(x, n):
    if n != 4:
        return [x] + [swap(x, "seq", k) for k in range(1, n)]
    far, near = swap(x, "seq", 2), swap(x, "seq", 1)
    return [x, near, far, swap(far, "seq", 1)]


def local(node_feats, qkv_weight, block_pairs, grad_out):
    feats = node_feats[0]
    rows, width = feats.shape
    n, m = lax.axis_size("seq"), lax.axis_size("clus")
    z, c = lax.axis_index("seq"), lax.axis_index("clus")
    plan = Plan(rows, qkv_weight.shape[0], n)
    nodes, heads = plan.nodes, plan.heads
    core = c % 2

    xs = gather_slots(feats, n)
    hcols = heads * HD

    def for_slot(k):
        return lax.dynamic_slice_in_dim(grad_out[0], (z ^ k) * hcols, hcols, 1)

    earlier = nodes - rows
    known_x, known = call(
        project_kernel,
        plan,
        [array(earlier, width), array(earlier, plan.columns)],
        [],
        2 * earlier * plan.columns * width,
        [*xs[:-1], qkv_weight],
    )

    own, *sent = after([for_slot(k) for k in range(n)], known)
    grads = [own] + [swap(sent[k - 1], "seq", k) for k in range(1, n)]

    per_dev = rows // BLOCK
    blocks = nodes // BLOCK
    listed = block_pairs[0]
    place = ((listed // per_dev) ^ z) * per_dev + listed % per_dev
    ids = jnp.arange(blocks, dtype=jnp.int32)
    row_ids = jnp.arange(2 * HD, dtype=jnp.int32) % HD
    allowed = jnp.any(
        (place[:, 0, None, None] == row_ids) & (place[:, 1, None, None] == ids[:, None]), axis=0
    )
    blocked = ~allowed & (row_ids < blocks)
    key_bias = jnp.repeat(jnp.where(blocked, NEVER, 0.0).astype(BF16), BLOCK, axis=0)
    row_hot = (jnp.arange(nodes, dtype=jnp.int32)[:, None] // BLOCK == row_ids).astype(BF16)

    def tiles(count):
        return [pltpu.VMEM((nodes, plan.tile), BF16)] * count

    low, sums, full, qkv = call(
        forward_kernel,
        plan,
        [array(heads, nodes, nodes), array(nodes, hcols, dtype=F32), array(nodes, width), array(nodes, plan.columns)],
        tiles(3) + [pltpu.VMEM((nodes, 2 * HD), BF16)],
        4 * nodes * nodes * HD * heads,
        [known, known_x, xs[-1], qkv_weight, key_bias, row_hot],
    )
    scratch = tiles(4) + [pltpu.VMEM((nodes, nodes), BF16), pltpu.VMEM((nodes, plan.tile), F32)]
    flops = 8 * nodes * nodes * HD * plan.gheads
    common = [qkv, *grads, low, sums]
    grad_t = []
    if plan.groups > 1:
        grad_other, wgrad_other = call(
            lambda *a: backward_kernel(a[0], True, *a[1:]),
            plan,
            [array(plan.gcols, nodes), array(plan.gcols, width)],
            scratch,
            flops + 2 * nodes * plan.gcols * width,
            [(1 - core).reshape(1), *common, full],
            scalar=True,
        )
        got = swap(wgrad_other, "clus", 1)
        grad_t = [grad_other]
    (grad_own,) = call(
        lambda *a: backward_kernel(a[0], False, *a[1:]),
        plan,
        [array(plan.gcols, nodes)],
        scratch,
        flops,
        [core.reshape(1), qkv, *grads, low, sums],
        scalar=True,
    )
    grad_t = [grad_own, *grad_t]
    count = 2 * nodes * plan.gcols * width
    half = plan.gcols // 2
    if plan.groups > 1:
        parts = call(
            weight_kernel, plan, [array(half, width)] * 2, [], count, [grad_own, full, got]
        )
    else:
        (wgrad,) = call(
            whole_weight_kernel, plan, [array(plan.gcols, width)], [], count, [grad_own, full]
        )
        keep = lax.dynamic_slice_in_dim(wgrad, core * half, half, 0)
        send = lax.dynamic_slice_in_dim(wgrad, (1 - core) * half, half, 0)
        parts = [add(keep, swap(send, "clus", 1))]
    sends = call(
        term_kernel,
        plan,
        [array(rows, width + hcols)] * n,
        [],
        count * plan.groups,
        [core.reshape(1), qkv_weight, sums, *grad_t],
        scalar=True,
    )
    if n == 4:
        ahead = swap(sends[3], "seq", 1)
        (pair,) = call(
            relay_kernel, plan, [array(rows, width + 2 * hcols)], [], 0, [sends[2], ahead]
        )
        received = [sends[0], swap(after(sends[1], ahead), "seq", 1), swap(pair, "seq", 2)]
    else:
        received = [sends[0]] + [swap(sends[k], "seq", k) for k in range(1, n)]

    bits = []
    while 2 << len(bits) < m:
        bits.append(2 << len(bits))

    def across(x, stage):
        pairs = [(i, i ^ (bits[-1 - stage] if i % 2 else bits[stage])) for i in range(m)]
        return lax.ppermute(x, "clus", pairs)

    def finish(parts, gots):
        parts = [add(part, got) for part, got in zip(parts, gots)]
        for stage in range(1, len(bits)):
            gots = [across(part, stage) for part in parts]
            parts = [add(part, got) for part, got in zip(parts, gots)]
        gots = [swap(part, "clus", 1) for part in parts]
        count, result = len(parts), None
        for i, (part, got) in enumerate(zip(parts, gots)):
            if i + 1 < count:
                places = [(True, i, count), (False, i, count)]
                result = scaled(plan, m, core, [part, got], places, result)
            else:
                result = scaled(plan, m, core, [part], [(True, i, count)], result)
                result = scaled(plan, m, core, [got], [(False, i, count)], result)
        return result

    gots = [across(part, 0) for part in parts]
    weight_grad = lax.cond(
        listed[0, 0] >= 0,
        finish,
        lambda parts, gots: jnp.zeros((plan.columns, width), F32),
        parts,
        gots,
    )

    received = after(received, weight_grad)
    aligned = hcols % 128 == 0
    node_grad, attended = call(
        combine_kernel,
        plan,
        [array(rows, width), array(rows, n * hcols) if aligned else array(n, rows, hcols)],
        [],
        0,
        [z.reshape(1), *received],
        scalar=True,
    )
    if not aligned:
        order = jnp.arange(n, dtype=jnp.int32) ^ z
        attended = attended[order].transpose(1, 0, 2).reshape(rows, n * hcols)
    return (attended[None], node_grad[None], weight_grad)


def solution(mesh):
    return jax.shard_map(
        local,
        mesh=mesh,
        in_specs=(
            P("clus", "seq", None),
            P("seq", None),
            P("clus", None, None),
            P("clus", "seq", None),
        ),
        out_specs=(P("clus", "seq", None), P("clus", "seq", None), P("seq", None)),
        check_vma=False,
    )
```

```python
import functools
import math

import jax
import jax.numpy as jnp
from jax import lax
from jax.experimental import pallas as pl
from jax.experimental.pallas import tpu as pltpu
from jax.sharding import PartitionSpec as P

HD = 64
BLOCK = 128
F32 = jnp.float32
BF16 = jnp.bfloat16
NT = (((1,), (1,)), ((), ()))
TN = (((0,), (0,)), ((), ()))
NEVER = -1e30
VMEM = pl.BlockSpec(memory_space=pltpu.VMEM)
HBM = pl.BlockSpec(memory_space=pltpu.HBM)
SMEM = pl.BlockSpec(memory_space=pltpu.SMEM)


def mm(a, b, dims=(((1,), (0,)), ((), ()))):
    return lax.dot_general(a, b, dims, preferred_element_type=F32)


class Plan:
    def __init__(self, rows, columns, n):
        self.n, self.rows, self.columns = n, rows, columns
        self.nodes = n * rows
        self.heads = columns // (3 * HD)
        self.groups = 2 if self.heads % 2 == 0 else 1
        self.gheads = self.heads // self.groups
        self.pair = self.gheads % 2 == 0
        self.per_tile = 2 if self.pair else 1
        self.tiles = self.gheads // self.per_tile
        self.tile = self.per_tile * HD
        self.gcols = self.gheads * 3 * HD
        self.chunk = math.gcd(self.nodes, 512)

    def base(self, group, t):
        start = group * self.gcols + t * 3 * self.tile
        return start if isinstance(start, int) else pl.multiple_of(start, self.tile)

    def feature(self, group, t):
        start = (group * self.tiles + t) * self.tile
        return start if isinstance(start, int) else pl.multiple_of(start, self.tile)


def low_half(shape):
    return lax.broadcasted_iota(jnp.int32, shape, 1) % (2 * HD) < HD


def first_kernel(plan, x, weight, weight_out, qkv, mark, sem):
    copy = pltpu.make_async_copy(weight, weight_out, sem)
    copy.start()
    copy.wait()
    qkv[...] = mm(x[...], weight_out[...], NT).astype(BF16)
    mark[...] = qkv[: mark.shape[0], : mark.shape[1]]


def project_kernel(plan, *refs):
    own, feats, (weight, qkv) = refs[0], refs[1:-2], refs[-2:]
    qkv[: plan.rows, :] = own[...]
    for s, x in enumerate(feats, 1):
        here = slice(s * plan.rows, (s + 1) * plan.rows)
        qkv[here, :] = mm(x[...], weight[...], NT).astype(BF16)


def load_tile(plan, qkv, group, t, q_s, k_s, v_s):
    base, tile = plan.base(group, t), plan.tile
    for s in range(plan.n):
        here = slice(s * plan.rows, (s + 1) * plan.rows)
        first, second, third = (qkv[here, pl.ds(base + i * tile, tile)] for i in range(3))
        if plan.pair:
            low = low_half(first.shape)
            queries = jnp.where(low, first, second)
            keys = pltpu.roll(jnp.where(low, third, first).astype(F32), HD, 1).astype(BF16)
            values = jnp.where(low, second, third)
        else:
            queries, keys, values = first, second, third
        q_s[here, :] = (queries.astype(F32) * HD ** -0.5).astype(BF16)
        k_s[here, :] = keys
        v_s[here, :] = values


def with_lanes(plan, h, x, extra):
    if not plan.pair:
        return jnp.concatenate([x, extra[:, :HD]], axis=1)
    low = low_half(x.shape)
    return jnp.where(low if h == 0 else ~low, x, extra)


def only_head(plan, h, x):
    if not plan.pair:
        return x
    low = low_half(x.shape)
    return jnp.where(low if h == 0 else ~low, x, jnp.zeros_like(x))


def merge(plan, h, x, before):
    if not plan.pair or h == 0:
        return x
    return jnp.where(low_half(x.shape), before, x)


def chunks(plan, body):
    steps = plan.nodes // plan.chunk
    if steps <= 4:
        for i in range(steps):
            body(i * plan.chunk)
    else:
        def step(i, carry):
            body(pl.multiple_of(i * plan.chunk, plan.chunk))
            return carry

        lax.fori_loop(0, steps, step, 0)


def forward_kernel(plan, *refs):
    n, rows = plan.n, plan.rows
    known, feats, (weight, key_bias, row_hot) = refs[0], refs[1 : 1 + n], refs[1 + n : 4 + n]
    low_ref, sum_ref, full_ref, qkv = refs[4 + n : 8 + n]
    pieces = refs[8 + n : -4]
    q_s, k_s, v_s, ka_s = refs[-4:]
    for s, x in enumerate(feats):
        full_ref[s * rows : (s + 1) * rows, :] = x[...]
    earlier = (n - 1) * rows
    qkv[:earlier, :] = known[...]
    qkv[earlier:, :] = mm(feats[-1][...], weight[...], NT).astype(BF16)
    for group in range(plan.groups):
        for t in range(plan.tiles):
            load_tile(plan, qkv, group, t, q_s, k_s, v_s)
            lanes = slice(plan.feature(group, t), plan.feature(group, t) + plan.tile)
            for h in range(plan.per_tile):
                head = (group * plan.tiles + t) * plan.per_tile + h
                ka_s[...] = with_lanes(plan, h, k_s[...], key_bias[...])

                def one_chunk(lo):
                    here = pl.ds(lo, plan.chunk)
                    queries = with_lanes(plan, h, q_s[here, :], row_hot[here, :])
                    scores = mm(queries, ka_s[...], NT)
                    unnorm = jnp.exp(scores - jnp.max(scores, axis=-1, keepdims=True))
                    low = (unnorm * (1.0 / jnp.sum(unnorm, axis=-1, keepdims=True))).astype(BF16)
                    low_ref[head, here, :] = low
                    sum_ref[here, lanes] = merge(plan, h, mm(low, v_s[...]), sum_ref[here, lanes])

                chunks(plan, one_chunk)
    for out in pieces:
        hcols = sum_ref.shape[1]
        for i in range(2):
            here = slice((2 + i) * rows, (3 + i) * rows)
            out[:, i * hcols : (i + 1) * hcols] = sum_ref[here, :].astype(BF16)


def backward_kernel(plan, with_weight, *refs):
    n, rows, tile = plan.n, plan.rows, plan.tile
    group = refs[0][0] if plan.groups > 1 else 0
    qkv, grads = refs[1], refs[2 : 2 + n]
    low_ref, sum_ref = refs[2 + n : 4 + n]
    at = 4 + n
    if with_weight:
        full_ref = refs[at]
        at += 1
    grad_ref = refs[at]
    at += 1
    if with_weight:
        wgrad_ref = refs[at]
        at += 1
    q_s, k_s, v_s, g_s, ds_s, dq_s = refs[at:]
    for t in range(plan.tiles):
        load_tile(plan, qkv, group, t, q_s, k_s, v_s)
        feature = plan.feature(group, t)
        for s in range(n):
            g_s[s * rows : (s + 1) * rows, :] = grads[s][:, pl.ds(feature, tile)]
        k_s[...] = (k_s[...].astype(F32) * HD ** -0.5).astype(BF16)
        q_t = q_s[...].T
        g_t = g_s[...].T
        for h in range(plan.per_tile):
            head = (group * plan.tiles + t) * plan.per_tile + h

            def one_chunk(lo):
                here = pl.ds(lo, plan.chunk)
                g_here = only_head(plan, h, g_s[here, :])
                delta = jnp.sum(
                    g_here.astype(F32) * sum_ref[here, pl.ds(feature, tile)], axis=-1, keepdims=True
                )
                grad_weights = mm(g_here, v_s[...], NT)
                ds = (low_ref[head, here, :].astype(F32) * (grad_weights - delta)).astype(BF16)
                ds_s[here, :] = ds
                dq_s[here, :] = merge(plan, h, mm(ds, k_s[...]), dq_s[here, :])

            chunks(plan, one_chunk)
            row = (t * plan.per_tile + h) * 3 * HD
            own = slice(h * HD, (h + 1) * HD)
            grad_ref[row + HD : row + 2 * HD, :] = mm(q_t[own, :], ds_s[...]).astype(BF16)
            grad_ref[row + 2 * HD : row + 3 * HD, :] = mm(g_t[own, :], low_ref[head]).astype(BF16)
        dq_t = dq_s[...].T.astype(BF16)
        for h in range(plan.per_tile):
            row = (t * plan.per_tile + h) * 3 * HD
            grad_ref[row : row + HD, :] = dq_t[h * HD : (h + 1) * HD, :]
    if with_weight:
        wgrad_ref[...] = mm(grad_ref[...], full_ref[...]).astype(BF16)


def weight_kernel(plan, grad_ref, full_ref, got_ref, *parts):
    size = parts[0].shape[0]
    for i, part in enumerate(parts):
        here = slice(i * size, (i + 1) * size)
        product = mm(grad_ref[here, :], full_ref[...])
        part[...] = (product + got_ref[here, :].astype(F32)).astype(BF16)


def whole_weight_kernel(plan, grad_ref, full_ref, wgrad_ref):
    wgrad_ref[...] = mm(grad_ref[...], full_ref[...]).astype(BF16)


def term_kernel(plan, slots, *refs):
    which, weight, sum_ref = refs[:3]
    grads = refs[3 : 3 + plan.groups]
    sends = refs[3 + plan.groups :]
    width = weight.shape[1]
    for s, out in zip(slots, sends):
        here = slice(s * plan.rows, (s + 1) * plan.rows)
        total = None
        for i, grad in enumerate(grads):
            if plan.groups > 1:
                group = which[0] if i == 0 else 1 - which[0]
                here_w = pl.ds(pl.multiple_of(group * plan.gcols, plan.gcols), plan.gcols)
            else:
                here_w = slice(None)
            part = mm(grad[:, here], weight[here_w, :], TN)
            total = part if total is None else total + part
        out[:, :width] = total.astype(BF16)
        if out.shape[1] > width:
            out[:, width:] = sum_ref[here, :].astype(BF16)


def scale_kernel(plan, m, places, which, *refs):
    out, staged, sems = refs[-3:]
    parts = refs[-3 - len(places) : -3]
    size = parts[0].shape[0]
    copies = []
    for i, (own, index, count) in enumerate(places):
        side = which[0] if own else 1 - which[0]
        start = pl.multiple_of((side * count + index) * size, size)
        staged[i] = parts[i][...].astype(F32) * (1.0 / m)
        copies.append(pltpu.make_async_copy(staged.at[i], out.at[pl.ds(start, size), :], sems.at[i]))
        copies[-1].start()
    for copy in copies:
        copy.wait()


def scaled(plan, m, core, parts, places, whole=None):
    rows, width = parts[0].shape
    count = len(parts)
    args = [core.reshape(1), *([] if whole is None else [whole]), *parts]
    specs = [SMEM] + [HBM] * (whole is not None) + [VMEM] * count
    return pl.pallas_call(
        functools.partial(scale_kernel, plan, m, places),
        out_shape=array(2 * places[0][2] * rows, width, dtype=F32),
        in_specs=specs,
        out_specs=HBM,
        scratch_shapes=[pltpu.VMEM((count, rows, width), F32), pltpu.SemaphoreType.DMA((count,))],
        input_output_aliases={} if whole is None else {1: 0},
        compiler_params=pltpu.CompilerParams(vmem_limit_bytes=12 * 2**20),
        cost_estimate=pl.CostEstimate(flops=0, bytes_accessed=1 << 20, transcendentals=0),
    )(*args)


def add_kernel(plan, one, other, out):
    out[...] = add(one[...], other[...])


def beside_kernel(plan, one, other, out):
    wide = one.shape[1]
    out[:, :wide] = one[...]
    out[:, wide:] = other[:, other.shape[1] // 2 :]


def combine_kernel(plan, pieces, place, *refs):
    hcols = plan.heads * HD
    received, (node_grad, attended) = refs[:-2], refs[-2:]
    width = node_grad.shape[1]
    total = received[0][:, :width].astype(F32)
    for x in received[1:]:
        if x.shape[1] >= width:
            total = total + x[:, :width].astype(F32)
    node_grad[...] = total.astype(BF16)
    for slot, (i, at) in enumerate(pieces):
        piece = received[i][:, at : at + hcols]
        if hcols % 128 == 0:
            start = pl.multiple_of((place[0] ^ slot) * hcols, hcols)
            attended[:, pl.ds(start, hcols)] = piece
        else:
            attended[slot, :, :] = piece


def size(x):
    return math.prod(x.shape) * jnp.dtype(x.dtype).itemsize


def call(kernel, plan, out_shape, scratch, flops, args, scalar=False, far=()):
    arrays = [x for x in scratch if hasattr(x, "dtype") and len(x.shape) > 0]
    held = sum(map(size, out_shape)) + sum(map(size, arrays)) + sum(map(size, args))
    held += 32 * plan.chunk * plan.nodes + 24 * plan.nodes * 2 * HD + 8 * 2**20
    return pl.pallas_call(
        functools.partial(kernel, plan),
        out_shape=out_shape,
        in_specs=[
            SMEM if scalar and i == 0 else HBM if i in far else VMEM for i in range(len(args))
        ],
        out_specs=[VMEM] * len(out_shape),
        scratch_shapes=scratch,
        compiler_params=pltpu.CompilerParams(vmem_limit_bytes=min(held, 60 * 2**20)),
        cost_estimate=pl.CostEstimate(flops=flops, bytes_accessed=4 << 20, transcendentals=0),
    )(*args)


def array(*shape, dtype=BF16):
    return jax.ShapeDtypeStruct(shape, dtype)


def swap(x, axis, bits):
    size = lax.axis_size(axis)
    return lax.ppermute(x, axis, [(i, i ^ bits) for i in range(size)])


def after(x, *done):
    return lax.optimization_barrier((x, *done))[0]


def add(a, b):
    return (a.astype(F32) + b.astype(F32)).astype(BF16)


def local(node_feats, qkv_weight, block_pairs, grad_out):
    feats = node_feats[0]
    rows, width = feats.shape
    n, m = lax.axis_size("seq"), lax.axis_size("clus")
    z, c = lax.axis_index("seq"), lax.axis_index("clus")
    plan = Plan(rows, qkv_weight.shape[0], n)
    nodes, heads = plan.nodes, plan.heads
    core = c % 2

    hcols = heads * HD

    def for_slot(k):
        return lax.dynamic_slice_in_dim(grad_out[0], (z ^ k) * hcols, hcols, 1)

    qkv_weight, own, mark = call(
        first_kernel,
        plan,
        [array(plan.columns, width), array(rows, plan.columns), array(16, 128)],
        [pltpu.SemaphoreType.DMA(())],
        2 * rows * plan.columns * width,
        [feats, qkv_weight],
        far=(1,),
    )
    if n == 4:
        far, near = swap(feats, "seq", 2), swap(feats, "seq", 1)
        xs = [feats, near, far, swap(after(far, mark), "seq", 1)]
    else:
        xs = [feats] + [swap(feats, "seq", k) for k in range(1, n)]
    earlier = nodes - rows
    (known,) = call(
        project_kernel,
        plan,
        [array(earlier, plan.columns)],
        [],
        2 * earlier * plan.columns * width,
        [own, *xs[1:-1], qkv_weight],
    )

    listed = block_pairs[0]
    always, known = lax.optimization_barrier((listed[0, 0] >= 0, known))
    mine, *sent = after([for_slot(k) for k in range(n)], known)
    grads = [mine] + [swap(sent[k - 1], "seq", k) for k in range(1, n)]

    per_dev = rows // BLOCK
    blocks = nodes // BLOCK
    place = ((listed // per_dev) ^ z) * per_dev + listed % per_dev
    ids = jnp.arange(blocks, dtype=jnp.int32)
    row_ids = jnp.arange(2 * HD, dtype=jnp.int32) % HD
    allowed = jnp.any(
        (place[:, 0, None, None] == row_ids) & (place[:, 1, None, None] == ids[:, None]), axis=0
    )
    blocked = ~allowed & (row_ids < blocks)
    key_bias = jnp.repeat(jnp.where(blocked, NEVER, 0.0).astype(BF16), BLOCK, axis=0)
    row_hot = (jnp.arange(nodes, dtype=jnp.int32)[:, None] // BLOCK == row_ids).astype(BF16)

    def tiles(count):
        return [pltpu.VMEM((nodes, plan.tile), BF16)] * count

    low, sums, full, qkv, *beyond = call(
        forward_kernel,
        plan,
        [array(heads, nodes, nodes), array(nodes, hcols, dtype=F32), array(nodes, width), array(nodes, plan.columns)]
        + [array(rows, 2 * hcols)] * (n == 4),
        tiles(3) + [pltpu.VMEM((nodes, 2 * HD), BF16)],
        4 * nodes * nodes * HD * heads,
        [known, *xs, qkv_weight, key_bias, row_hot],
    )
    scratch = tiles(4) + [pltpu.VMEM((nodes, nodes), BF16), pltpu.VMEM((nodes, plan.tile), F32)]
    flops = 8 * nodes * nodes * HD * plan.gheads
    common = [qkv, *grads, low, sums]
    grad_t = []
    if plan.groups > 1:
        grad_other, wgrad_other = call(
            lambda *a: backward_kernel(a[0], True, *a[1:]),
            plan,
            [array(plan.gcols, nodes), array(plan.gcols, width)],
            scratch,
            flops + 2 * nodes * plan.gcols * width,
            [(1 - core).reshape(1), *common, full],
            scalar=True,
        )
        got = swap(wgrad_other, "clus", 1)
        grad_t = [grad_other]
    (grad_own,) = call(
        lambda *a: backward_kernel(a[0], False, *a[1:]),
        plan,
        [array(plan.gcols, nodes)],
        scratch,
        flops,
        [core.reshape(1), qkv, *grads, low, sums],
        scalar=True,
    )
    grad_t = [grad_own, *grad_t]
    count = 2 * nodes * plan.gcols * width
    half = plan.gcols // 2
    if plan.groups > 1:
        parts = call(
            weight_kernel, plan, [array(half, width)] * 2, [], count, [grad_own, full, got]
        )
    else:
        (wgrad,) = call(
            whole_weight_kernel, plan, [array(plan.gcols, width)], [], count, [grad_own, full]
        )
        keep = lax.dynamic_slice_in_dim(wgrad, core * half, half, 0)
        send = lax.dynamic_slice_in_dim(wgrad, (1 - core) * half, half, 0)
        parts = [add(keep, swap(send, "clus", 1))]
    def terms(slots, wide, *done):
        return call(
            lambda *a: term_kernel(a[0], slots, *a[1:]),
            plan,
            [array(rows, width + hcols * extra) for extra in wide],
            [],
            count * plan.groups * len(slots) // n,
            [core.reshape(1), qkv_weight, after(sums, *done), *grad_t],
            scalar=True,
        )

    if n == 4:
        (ahead,) = terms([3], [0])
        ahead = swap(ahead, "seq", 1)
        own_term, near, far_term = terms([0, 1, 2], [1, 1, 0], parts)
        across_z = swap(after(beyond[0], parts), "seq", 2)
        (pair,) = call(add_kernel, plan, [array(rows, width)], [], 0, [far_term, ahead])
        (near,) = call(
            beside_kernel,
            plan,
            [array(rows, width + 2 * hcols)],
            [],
            0,
            [near, across_z],
        )
        received = [own_term, swap(near, "seq", 1), swap(pair, "seq", 2), across_z]
        places = [(0, width), (1, width), (3, 0), (1, width + hcols)]
    else:
        sends = terms(range(n), [1] * n)
        received = [sends[0]] + [swap(sends[k], "seq", k) for k in range(1, n)]
        places = [(k, width) for k in range(n)]

    bits = []
    while 2 << len(bits) < m:
        bits.append(2 << len(bits))

    def across(x, stage):
        pairs = [(i, i ^ (bits[-1 - stage] if i % 2 else bits[stage])) for i in range(m)]
        return lax.ppermute(x, "clus", pairs)

    def finish(parts, gots):
        parts = [add(part, got) for part, got in zip(parts, gots)]
        for stage in range(1, len(bits)):
            gots = [across(part, stage) for part in parts]
            parts = [add(part, got) for part, got in zip(parts, gots)]
        gots = [swap(part, "clus", 1) for part in parts]
        count, result = len(parts), None
        for i, (part, got) in enumerate(zip(parts, gots)):
            if i + 1 < count:
                places = [(True, i, count), (False, i, count)]
                result = scaled(plan, m, core, [part, got], places, result)
            else:
                result = scaled(plan, m, core, [part], [(True, i, count)], result)
                result = scaled(plan, m, core, [got], [(False, i, count)], result)
        return result

    gots = [across(part, 0) for part in parts]
    weight_grad = lax.cond(
        always,
        finish,
        lambda parts, gots: jnp.zeros((plan.columns, width), F32),
        parts,
        gots,
    )

    received = after(received, weight_grad)
    aligned = hcols % 128 == 0
    node_grad, attended = call(
        lambda *a: combine_kernel(a[0], places, *a[1:]),
        plan,
        [array(rows, width), array(rows, n * hcols) if aligned else array(n, rows, hcols)],
        [],
        0,
        [z.reshape(1), *received],
        scalar=True,
    )
    if not aligned:
        order = jnp.arange(n, dtype=jnp.int32) ^ z
        attended = attended[order].transpose(1, 0, 2).reshape(rows, n * hcols)
    return (attended[None], node_grad[None], weight_grad)


def solution(mesh):
    return jax.shard_map(
        local,
        mesh=mesh,
        in_specs=(
            P("clus", "seq", None),
            P("seq", None),
            P("clus", None, None),
            P("clus", "seq", None),
        ),
        out_specs=(P("clus", "seq", None), P("clus", "seq", None), P("seq", None)),
        check_vma=False,
    )
```

```python
import functools
import math

import jax
import jax.numpy as jnp
from jax import lax
from jax.experimental import pallas as pl
from jax.experimental.pallas import tpu as pltpu
from jax.sharding import PartitionSpec as P

HD = 64
BLOCK = 128
F32 = jnp.float32
BF16 = jnp.bfloat16
NT = (((1,), (1,)), ((), ()))
TN = (((0,), (0,)), ((), ()))
NEVER = -1e30
VMEM = pl.BlockSpec(memory_space=pltpu.VMEM)
HBM = pl.BlockSpec(memory_space=pltpu.HBM)
SMEM = pl.BlockSpec(memory_space=pltpu.SMEM)


def mm(a, b, dims=(((1,), (0,)), ((), ()))):
    return lax.dot_general(a, b, dims, preferred_element_type=F32)


class Plan:
    def __init__(self, rows, columns, n):
        self.n, self.rows, self.columns = n, rows, columns
        self.nodes = n * rows
        self.heads = columns // (3 * HD)
        self.groups = 2 if self.heads % 2 == 0 else 1
        self.gheads = self.heads // self.groups
        self.pair = self.gheads % 2 == 0
        self.per_tile = 2 if self.pair else 1
        self.tiles = self.gheads // self.per_tile
        self.tile = self.per_tile * HD
        self.gcols = self.gheads * 3 * HD
        self.chunk = math.gcd(self.nodes, 512)

    def base(self, group, t):
        start = group * self.gcols + t * 3 * self.tile
        return start if isinstance(start, int) else pl.multiple_of(start, self.tile)

    def feature(self, group, t):
        start = (group * self.tiles + t) * self.tile
        return start if isinstance(start, int) else pl.multiple_of(start, self.tile)


def low_half(shape):
    return lax.broadcasted_iota(jnp.int32, shape, 1) % (2 * HD) < HD


def first_kernel(plan, x, weight, weight_out, qkv, mark, sem):
    copy = pltpu.make_async_copy(weight, weight_out, sem)
    copy.start()
    copy.wait()
    qkv[...] = mm(x[...], weight_out[...], NT).astype(BF16)
    mark[...] = qkv[: mark.shape[0], : mark.shape[1]]


def project_kernel(plan, *refs):
    own, feats, (weight, qkv) = refs[0], refs[-3:0:-1], refs[-2:]
    qkv[: plan.rows, :] = own[...]
    for s, x in enumerate(feats, 1):
        here = slice(s * plan.rows, (s + 1) * plan.rows)
        qkv[here, :] = mm(x[...], weight[...], NT).astype(BF16)


def load_tile(plan, qkv, group, t, q_s, k_s, v_s):
    base, tile = plan.base(group, t), plan.tile
    for s in range(plan.n):
        here = slice(s * plan.rows, (s + 1) * plan.rows)
        first, second, third = (qkv[here, pl.ds(base + i * tile, tile)] for i in range(3))
        if plan.pair:
            low = low_half(first.shape)
            queries = jnp.where(low, first, second)
            keys = pltpu.roll(jnp.where(low, third, first).astype(F32), HD, 1).astype(BF16)
            values = jnp.where(low, second, third)
        else:
            queries, keys, values = first, second, third
        q_s[here, :] = (queries.astype(F32) * HD ** -0.5).astype(BF16)
        k_s[here, :] = keys
        v_s[here, :] = values


def with_lanes(plan, h, x, extra):
    if not plan.pair:
        return jnp.concatenate([x, extra[:, :HD]], axis=1)
    low = low_half(x.shape)
    return jnp.where(low if h == 0 else ~low, x, extra)


def only_head(plan, h, x):
    if not plan.pair:
        return x
    low = low_half(x.shape)
    return jnp.where(low if h == 0 else ~low, x, jnp.zeros_like(x))


def merge(plan, h, x, before):
    if not plan.pair or h == 0:
        return x
    return jnp.where(low_half(x.shape), before, x)


def chunks(plan, body):
    steps = plan.nodes // plan.chunk
    if steps <= 4:
        for i in range(steps):
            body(i * plan.chunk)
    else:
        def step(i, carry):
            body(pl.multiple_of(i * plan.chunk, plan.chunk))
            return carry

        lax.fori_loop(0, steps, step, 0)


def forward_kernel(plan, *refs):
    n, rows = plan.n, plan.rows
    known, feats, (weight, key_bias, row_hot) = refs[0], refs[1 : 1 + n], refs[1 + n : 4 + n]
    low_ref, sum_ref, full_ref, qkv = refs[4 + n : 8 + n]
    pieces = refs[8 + n : -4]
    q_s, k_s, v_s, ka_s = refs[-4:]
    for s, x in enumerate(feats):
        full_ref[s * rows : (s + 1) * rows, :] = x[...]
    earlier = (n - 1) * rows
    qkv[:earlier, :] = known[...]
    qkv[earlier:, :] = mm(feats[-1][...], weight[...], NT).astype(BF16)
    for group in range(plan.groups):
        for t in range(plan.tiles):
            load_tile(plan, qkv, group, t, q_s, k_s, v_s)
            lanes = slice(plan.feature(group, t), plan.feature(group, t) + plan.tile)
            for h in range(plan.per_tile):
                head = (group * plan.tiles + t) * plan.per_tile + h
                ka_s[...] = with_lanes(plan, h, k_s[...], key_bias[...])

                def one_chunk(lo):
                    here = pl.ds(lo, plan.chunk)
                    queries = with_lanes(plan, h, q_s[here, :], row_hot[here, :])
                    scores = mm(queries, ka_s[...], NT)
                    unnorm = jnp.exp(scores - jnp.max(scores, axis=-1, keepdims=True))
                    low = (unnorm * (1.0 / jnp.sum(unnorm, axis=-1, keepdims=True))).astype(BF16)
                    low_ref[head, here, :] = low
                    sum_ref[here, lanes] = merge(plan, h, mm(low, v_s[...]), sum_ref[here, lanes])

                chunks(plan, one_chunk)
    for out in pieces:
        hcols = sum_ref.shape[1]
        for i in range(2):
            here = slice((2 + i) * rows, (3 + i) * rows)
            out[:, i * hcols : (i + 1) * hcols] = sum_ref[here, :].astype(BF16)


def backward_kernel(plan, with_weight, *refs):
    n, rows, tile = plan.n, plan.rows, plan.tile
    group = refs[0][0] if plan.groups > 1 else 0
    qkv, grads = refs[1], refs[2 : 2 + n]
    low_ref, sum_ref = refs[2 + n : 4 + n]
    at = 4 + n
    if with_weight:
        full_ref = refs[at]
        at += 1
    grad_ref = refs[at]
    at += 1
    if with_weight:
        wgrad_ref = refs[at]
        at += 1
    q_s, k_s, v_s, g_s, ds_s, dq_s = refs[at:]
    for t in range(plan.tiles):
        load_tile(plan, qkv, group, t, q_s, k_s, v_s)
        feature = plan.feature(group, t)
        for s in range(n):
            g_s[s * rows : (s + 1) * rows, :] = grads[s][:, pl.ds(feature, tile)]
        k_s[...] = (k_s[...].astype(F32) * HD ** -0.5).astype(BF16)
        q_t = q_s[...].T
        g_t = g_s[...].T
        for h in range(plan.per_tile):
            head = (group * plan.tiles + t) * plan.per_tile + h

            def one_chunk(lo):
                here = pl.ds(lo, plan.chunk)
                g_here = only_head(plan, h, g_s[here, :])
                delta = jnp.sum(
                    g_here.astype(F32) * sum_ref[here, pl.ds(feature, tile)], axis=-1, keepdims=True
                )
                grad_weights = mm(g_here, v_s[...], NT)
                ds = (low_ref[head, here, :].astype(F32) * (grad_weights - delta)).astype(BF16)
                ds_s[here, :] = ds
                dq_s[here, :] = merge(plan, h, mm(ds, k_s[...]), dq_s[here, :])

            chunks(plan, one_chunk)
            row = (t * plan.per_tile + h) * 3 * HD
            own = slice(h * HD, (h + 1) * HD)
            grad_ref[row + HD : row + 2 * HD, :] = mm(q_t[own, :], ds_s[...]).astype(BF16)
            grad_ref[row + 2 * HD : row + 3 * HD, :] = mm(g_t[own, :], low_ref[head]).astype(BF16)
        dq_t = dq_s[...].T.astype(BF16)
        for h in range(plan.per_tile):
            row = (t * plan.per_tile + h) * 3 * HD
            grad_ref[row : row + HD, :] = dq_t[h * HD : (h + 1) * HD, :]
    if with_weight:
        wgrad_ref[...] = mm(grad_ref[...], full_ref[...]).astype(BF16)


def weight_kernel(plan, grad_ref, full_ref, got_ref, *parts):
    size = parts[0].shape[0]
    for i, part in enumerate(parts):
        here = slice(i * size, (i + 1) * size)
        product = mm(grad_ref[here, :], full_ref[...])
        part[...] = (product + got_ref[here, :].astype(F32)).astype(BF16)


def whole_weight_kernel(plan, grad_ref, full_ref, wgrad_ref):
    wgrad_ref[...] = mm(grad_ref[...], full_ref[...]).astype(BF16)


def term_kernel(plan, slots, *refs):
    which, weight, sum_ref = refs[:3]
    grads = refs[3 : 3 + plan.groups]
    sends = refs[3 + plan.groups :]
    width = weight.shape[1]
    for s, out in zip(slots, sends):
        here = slice(s * plan.rows, (s + 1) * plan.rows)
        total = None
        for i, grad in enumerate(grads):
            if plan.groups > 1:
                group = which[0] if i == 0 else 1 - which[0]
                here_w = pl.ds(pl.multiple_of(group * plan.gcols, plan.gcols), plan.gcols)
            else:
                here_w = slice(None)
            part = mm(grad[:, here], weight[here_w, :], TN)
            total = part if total is None else total + part
        out[:, :width] = total.astype(BF16)
        if out.shape[1] > width:
            out[:, width:] = sum_ref[here, :].astype(BF16)


def scale_kernel(plan, m, places, which, *refs):
    out, staged, sems = refs[-3:]
    parts = refs[-3 - len(places) : -3]
    size = parts[0].shape[0]
    copies = []
    for i, (own, index, count) in enumerate(places):
        side = which[0] if own else 1 - which[0]
        start = pl.multiple_of((side * count + index) * size, size)
        staged[i] = parts[i][...].astype(F32) * (1.0 / m)
        copies.append(pltpu.make_async_copy(staged.at[i], out.at[pl.ds(start, size), :], sems.at[i]))
        copies[-1].start()
    for copy in copies:
        copy.wait()


def scaled(plan, m, core, parts, places, whole=None):
    rows, width = parts[0].shape
    count = len(parts)
    args = [core.reshape(1), *([] if whole is None else [whole]), *parts]
    specs = [SMEM] + [HBM] * (whole is not None) + [VMEM] * count
    return pl.pallas_call(
        functools.partial(scale_kernel, plan, m, places),
        out_shape=array(2 * places[0][2] * rows, width, dtype=F32),
        in_specs=specs,
        out_specs=HBM,
        scratch_shapes=[pltpu.VMEM((count, rows, width), F32), pltpu.SemaphoreType.DMA((count,))],
        input_output_aliases={} if whole is None else {1: 0},
        compiler_params=pltpu.CompilerParams(vmem_limit_bytes=12 * 2**20),
        cost_estimate=pl.CostEstimate(flops=0, bytes_accessed=1 << 20, transcendentals=0),
    )(*args)


def add_kernel(plan, one, other, out):
    out[...] = add(one[...], other[...])


def beside_kernel(plan, one, other, out):
    wide = one.shape[1]
    out[:, :wide] = one[...]
    out[:, wide:] = other[:, other.shape[1] // 2 :]


def combine_kernel(plan, pieces, place, *refs):
    hcols = plan.heads * HD
    received, (node_grad, attended) = refs[:-2], refs[-2:]
    width = node_grad.shape[1]
    total = received[0][:, :width].astype(F32)
    for x in received[1:]:
        if x.shape[1] >= width:
            total = total + x[:, :width].astype(F32)
    node_grad[...] = total.astype(BF16)
    for slot, (i, at) in enumerate(pieces):
        piece = received[i][:, at : at + hcols]
        if hcols % 128 == 0:
            start = pl.multiple_of((place[0] ^ slot) * hcols, hcols)
            attended[:, pl.ds(start, hcols)] = piece
        else:
            attended[slot, :, :] = piece


def size(x):
    return math.prod(x.shape) * jnp.dtype(x.dtype).itemsize


def call(kernel, plan, out_shape, scratch, flops, args, scalar=False, far=()):
    arrays = [x for x in scratch if hasattr(x, "dtype") and len(x.shape) > 0]
    held = sum(map(size, out_shape)) + sum(map(size, arrays)) + sum(map(size, args))
    held += 32 * plan.chunk * plan.nodes + 24 * plan.nodes * 2 * HD + 8 * 2**20
    return pl.pallas_call(
        functools.partial(kernel, plan),
        out_shape=out_shape,
        in_specs=[
            SMEM if scalar and i == 0 else HBM if i in far else VMEM for i in range(len(args))
        ],
        out_specs=[VMEM] * len(out_shape),
        scratch_shapes=scratch,
        compiler_params=pltpu.CompilerParams(vmem_limit_bytes=min(held, 60 * 2**20)),
        cost_estimate=pl.CostEstimate(flops=flops, bytes_accessed=4 << 20, transcendentals=0),
    )(*args)


def array(*shape, dtype=BF16):
    return jax.ShapeDtypeStruct(shape, dtype)


def swap(x, axis, bits):
    size = lax.axis_size(axis)
    return lax.ppermute(x, axis, [(i, i ^ bits) for i in range(size)])


def after(x, *done):
    return lax.optimization_barrier((x, *done))[0]


def add(a, b):
    return (a.astype(F32) + b.astype(F32)).astype(BF16)


def local(node_feats, qkv_weight, block_pairs, grad_out):
    feats = node_feats[0]
    rows, width = feats.shape
    n, m = lax.axis_size("seq"), lax.axis_size("clus")
    z, c = lax.axis_index("seq"), lax.axis_index("clus")
    plan = Plan(rows, qkv_weight.shape[0], n)
    nodes, heads = plan.nodes, plan.heads
    core = c % 2

    hcols = heads * HD

    def for_slot(k):
        return lax.dynamic_slice_in_dim(grad_out[0], (z ^ k) * hcols, hcols, 1)

    qkv_weight, own, mark = call(
        first_kernel,
        plan,
        [array(plan.columns, width), array(rows, plan.columns), array(16, 128)],
        [pltpu.SemaphoreType.DMA(())],
        2 * rows * plan.columns * width,
        [feats, qkv_weight],
        far=(1,),
    )
    if n == 4:
        far, near = swap(feats, "seq", 2), swap(feats, "seq", 1)
        xs = [feats, near, far, swap(after(far, mark), "seq", 1)]
    else:
        xs = [feats] + [swap(feats, "seq", k) for k in range(1, n)]
    earlier = nodes - rows
    (known,) = call(
        project_kernel,
        plan,
        [array(earlier, plan.columns)],
        [],
        2 * earlier * plan.columns * width,
        [own, *xs[-2:0:-1], qkv_weight],
    )

    listed = block_pairs[0]
    always, known = lax.optimization_barrier((listed[0, 0] >= 0, known))
    mine, *sent = after([for_slot(k) for k in range(n)], known)
    grads = [mine] + [swap(sent[k - 1], "seq", k) for k in range(1, n)]

    per_dev = rows // BLOCK
    blocks = nodes // BLOCK
    place = ((listed // per_dev) ^ z) * per_dev + listed % per_dev
    ids = jnp.arange(blocks, dtype=jnp.int32)
    row_ids = jnp.arange(2 * HD, dtype=jnp.int32) % HD
    allowed = jnp.any(
        (place[:, 0, None, None] == row_ids) & (place[:, 1, None, None] == ids[:, None]), axis=0
    )
    blocked = ~allowed & (row_ids < blocks)
    key_bias = jnp.repeat(jnp.where(blocked, NEVER, 0.0).astype(BF16), BLOCK, axis=0)
    row_hot = (jnp.arange(nodes, dtype=jnp.int32)[:, None] // BLOCK == row_ids).astype(BF16)

    def tiles(count):
        return [pltpu.VMEM((nodes, plan.tile), BF16)] * count

    low, sums, full, qkv, *beyond = call(
        forward_kernel,
        plan,
        [array(heads, nodes, nodes), array(nodes, hcols, dtype=F32), array(nodes, width), array(nodes, plan.columns)]
        + [array(rows, 2 * hcols)] * (n == 4),
        tiles(3) + [pltpu.VMEM((nodes, 2 * HD), BF16)],
        4 * nodes * nodes * HD * heads,
        [known, *xs, qkv_weight, key_bias, row_hot],
    )
    scratch = tiles(4) + [pltpu.VMEM((nodes, nodes), BF16), pltpu.VMEM((nodes, plan.tile), F32)]
    flops = 8 * nodes * nodes * HD * plan.gheads
    common = [qkv, *grads, low, sums]
    grad_t = []
    if plan.groups > 1:
        grad_other, wgrad_other = call(
            lambda *a: backward_kernel(a[0], True, *a[1:]),
            plan,
            [array(plan.gcols, nodes), array(plan.gcols, width)],
            scratch,
            flops + 2 * nodes * plan.gcols * width,
            [(1 - core).reshape(1), *common, full],
            scalar=True,
        )
        got = swap(wgrad_other, "clus", 1)
        grad_t = [grad_other]
    (grad_own,) = call(
        lambda *a: backward_kernel(a[0], False, *a[1:]),
        plan,
        [array(plan.gcols, nodes)],
        scratch,
        flops,
        [core.reshape(1), qkv, *grads, low, sums],
        scalar=True,
    )
    grad_t = [grad_own, *grad_t]
    count = 2 * nodes * plan.gcols * width
    half = plan.gcols // 2
    if plan.groups > 1:
        parts = call(
            weight_kernel, plan, [array(half, width)] * 2, [], count, [grad_own, full, got]
        )
    else:
        (wgrad,) = call(
            whole_weight_kernel, plan, [array(plan.gcols, width)], [], count, [grad_own, full]
        )
        keep = lax.dynamic_slice_in_dim(wgrad, core * half, half, 0)
        send = lax.dynamic_slice_in_dim(wgrad, (1 - core) * half, half, 0)
        parts = [add(keep, swap(send, "clus", 1))]
    def terms(slots, wide, *done):
        return call(
            lambda *a: term_kernel(a[0], slots, *a[1:]),
            plan,
            [array(rows, width + hcols * extra) for extra in wide],
            [],
            count * plan.groups * len(slots) // n,
            [core.reshape(1), qkv_weight, after(sums, *done), *grad_t],
            scalar=True,
        )

    if n == 4:
        (ahead,) = terms([3], [0])
        ahead = swap(ahead, "seq", 1)
        own_term, near, far_term = terms([0, 1, 2], [1, 1, 0], parts)
        across_z = swap(after(beyond[0], parts), "seq", 2)
        (pair,) = call(add_kernel, plan, [array(rows, width)], [], 0, [far_term, ahead])
        (near,) = call(
            beside_kernel,
            plan,
            [array(rows, width + 2 * hcols)],
            [],
            0,
            [near, across_z],
        )
        received = [own_term, swap(near, "seq", 1), swap(pair, "seq", 2), across_z]
        places = [(0, width), (1, width), (3, 0), (1, width + hcols)]
    else:
        sends = terms(range(n), [1] * n)
        received = [sends[0]] + [swap(sends[k], "seq", k) for k in range(1, n)]
        places = [(k, width) for k in range(n)]

    bits = []
    while 2 << len(bits) < m:
        bits.append(2 << len(bits))

    def across(x, stage):
        pairs = [(i, i ^ (bits[-1 - stage] if i % 2 else bits[stage])) for i in range(m)]
        return lax.ppermute(x, "clus", pairs)

    def finish(parts, gots):
        parts = [add(part, got) for part, got in zip(parts, gots)]
        for stage in range(1, len(bits)):
            gots = [across(part, stage) for part in parts]
            parts = [add(part, got) for part, got in zip(parts, gots)]
        gots = [swap(part, "clus", 1) for part in parts]
        held, places = [], []
        for i, (part, got) in enumerate(zip(parts, gots)):
            held += [part, got]
            places += [(True, i, len(parts)), (False, i, len(parts))]
        result = scaled(plan, m, core, held[:-1], places[:-1])
        result = scaled(plan, m, core, held[-1:], places[-1:], result)
        return result

    gots = [across(part, 0) for part in parts]
    weight_grad = lax.cond(
        always,
        finish,
        lambda parts, gots: jnp.zeros((plan.columns, width), F32),
        parts,
        gots,
    )

    received = after(received, weight_grad)
    aligned = hcols % 128 == 0
    node_grad, attended = call(
        lambda *a: combine_kernel(a[0], places, *a[1:]),
        plan,
        [array(rows, width), array(rows, n * hcols) if aligned else array(n, rows, hcols)],
        [],
        0,
        [z.reshape(1), *received],
        scalar=True,
    )
    if not aligned:
        order = jnp.arange(n, dtype=jnp.int32) ^ z
        attended = attended[order].transpose(1, 0, 2).reshape(rows, n * hcols)
    return (attended[None], node_grad[None], weight_grad)


def solution(mesh):
    return jax.shard_map(
        local,
        mesh=mesh,
        in_specs=(
            P("clus", "seq", None),
            P("seq", None),
            P("clus", None, None),
            P("clus", "seq", None),
        ),
        out_specs=(P("clus", "seq", None), P("clus", "seq", None), P("seq", None)),
        check_vma=False,
    )
```

```python
import functools
import math

import jax
import jax.numpy as jnp
from jax import lax
from jax.experimental import pallas as pl
from jax.experimental.pallas import tpu as pltpu
from jax.sharding import PartitionSpec as P

HD = 64
BLOCK = 128
F32 = jnp.float32
BF16 = jnp.bfloat16
NT = (((1,), (1,)), ((), ()))
TN = (((0,), (0,)), ((), ()))
NEVER = -1e30
VMEM = pl.BlockSpec(memory_space=pltpu.VMEM)
HBM = pl.BlockSpec(memory_space=pltpu.HBM)
SMEM = pl.BlockSpec(memory_space=pltpu.SMEM)


def mm(a, b, dims=(((1,), (0,)), ((), ()))):
    return lax.dot_general(a, b, dims, preferred_element_type=F32)


class Plan:
    def __init__(self, rows, columns, n):
        self.n, self.rows, self.columns = n, rows, columns
        self.nodes = n * rows
        self.heads = columns // (3 * HD)
        self.groups = 2 if self.heads % 2 == 0 else 1
        self.gheads = self.heads // self.groups
        self.pair = self.gheads % 2 == 0
        self.per_tile = 2 if self.pair else 1
        self.tiles = self.gheads // self.per_tile
        self.tile = self.per_tile * HD
        self.gcols = self.gheads * 3 * HD
        self.chunk = math.gcd(self.nodes, 512)

    def base(self, group, t):
        start = group * self.gcols + t * 3 * self.tile
        return start if isinstance(start, int) else pl.multiple_of(start, self.tile)

    def feature(self, group, t):
        start = (group * self.tiles + t) * self.tile
        return start if isinstance(start, int) else pl.multiple_of(start, self.tile)


def low_half(shape):
    return lax.broadcasted_iota(jnp.int32, shape, 1) % (2 * HD) < HD


def first_kernel(plan, x, weight, weight_out, qkv, mark, sem):
    copy = pltpu.make_async_copy(weight, weight_out, sem)
    copy.start()
    copy.wait()
    qkv[...] = mm(x[...], weight_out[...], NT).astype(BF16)
    mark[...] = qkv[: mark.shape[0], : mark.shape[1]]


def project_kernel(plan, *refs):
    own, feats, (weight, qkv) = refs[0], refs[-3:0:-1], refs[-2:]
    qkv[: plan.rows, :] = own[...]
    for s, x in enumerate(feats, 1):
        here = slice(s * plan.rows, (s + 1) * plan.rows)
        qkv[here, :] = mm(x[...], weight[...], NT).astype(BF16)


def load_tile(plan, qkv, group, t, q_s, k_s, v_s):
    base, tile = plan.base(group, t), plan.tile
    for s in range(plan.n):
        here = slice(s * plan.rows, (s + 1) * plan.rows)
        first, second, third = (qkv[here, pl.ds(base + i * tile, tile)] for i in range(3))
        if plan.pair:
            low = low_half(first.shape)
            queries = jnp.where(low, first, second)
            keys = pltpu.roll(jnp.where(low, third, first).astype(F32), HD, 1).astype(BF16)
            values = jnp.where(low, second, third)
        else:
            queries, keys, values = first, second, third
        q_s[here, :] = (queries.astype(F32) * HD ** -0.5).astype(BF16)
        k_s[here, :] = keys
        v_s[here, :] = values


def with_lanes(plan, h, x, extra):
    if not plan.pair:
        return jnp.concatenate([x, extra[:, :HD]], axis=1)
    low = low_half(x.shape)
    return jnp.where(low if h == 0 else ~low, x, extra)


def only_head(plan, h, x):
    if not plan.pair:
        return x
    low = low_half(x.shape)
    return jnp.where(low if h == 0 else ~low, x, jnp.zeros_like(x))


def merge(plan, h, x, before):
    if not plan.pair or h == 0:
        return x
    return jnp.where(low_half(x.shape), before, x)


def chunks(plan, body):
    steps = plan.nodes // plan.chunk
    if steps <= 4:
        for i in range(steps):
            body(i * plan.chunk)
    else:
        def step(i, carry):
            body(pl.multiple_of(i * plan.chunk, plan.chunk))
            return carry

        lax.fori_loop(0, steps, step, 0)


def forward_kernel(plan, *refs):
    n, rows = plan.n, plan.rows
    known, feats, (weight, key_bias, row_hot) = refs[0], refs[1 : 1 + n], refs[1 + n : 4 + n]
    low_ref, sum_ref, full_ref, qkv = refs[4 + n : 8 + n]
    q_s, k_s, v_s, ka_s = refs[-4:]
    for s, x in enumerate(feats):
        full_ref[s * rows : (s + 1) * rows, :] = x[...]
    earlier = (n - 1) * rows
    qkv[:earlier, :] = known[...]
    qkv[earlier:, :] = mm(feats[-1][...], weight[...], NT).astype(BF16)
    for group in range(plan.groups):
        for t in range(plan.tiles):
            load_tile(plan, qkv, group, t, q_s, k_s, v_s)
            lanes = slice(plan.feature(group, t), plan.feature(group, t) + plan.tile)
            for h in range(plan.per_tile):
                head = (group * plan.tiles + t) * plan.per_tile + h
                ka_s[...] = with_lanes(plan, h, k_s[...], key_bias[...])

                def one_chunk(lo):
                    here = pl.ds(lo, plan.chunk)
                    queries = with_lanes(plan, h, q_s[here, :], row_hot[here, :])
                    scores = mm(queries, ka_s[...], NT)
                    unnorm = jnp.exp(scores - jnp.max(scores, axis=-1, keepdims=True))
                    low = (unnorm * (1.0 / jnp.sum(unnorm, axis=-1, keepdims=True))).astype(BF16)
                    low_ref[head, here, :] = low
                    sum_ref[here, lanes] = merge(plan, h, mm(low, v_s[...]), sum_ref[here, lanes])

                chunks(plan, one_chunk)


def backward_kernel(plan, with_weight, *refs):
    n, rows, tile = plan.n, plan.rows, plan.tile
    group = refs[0][0] if plan.groups > 1 else 0
    qkv, grads = refs[1], refs[2 : 2 + n]
    low_ref, sum_ref = refs[2 + n : 4 + n]
    at = 4 + n
    if with_weight:
        full_ref = refs[at]
        at += 1
    grad_ref = refs[at]
    at += 1
    if with_weight:
        wgrad_ref = refs[at]
        at += 1
    q_s, k_s, v_s, g_s, ds_s, dq_s = refs[at:]
    for t in range(plan.tiles):
        load_tile(plan, qkv, group, t, q_s, k_s, v_s)
        feature = plan.feature(group, t)
        for s in range(n):
            g_s[s * rows : (s + 1) * rows, :] = grads[s][:, pl.ds(feature, tile)]
        k_s[...] = (k_s[...].astype(F32) * HD ** -0.5).astype(BF16)
        q_t = q_s[...].T
        g_t = g_s[...].T
        for h in range(plan.per_tile):
            head = (group * plan.tiles + t) * plan.per_tile + h

            def one_chunk(lo):
                here = pl.ds(lo, plan.chunk)
                g_here = only_head(plan, h, g_s[here, :])
                delta = jnp.sum(
                    g_here.astype(F32) * sum_ref[here, pl.ds(feature, tile)], axis=-1, keepdims=True
                )
                grad_weights = mm(g_here, v_s[...], NT)
                ds = (low_ref[head, here, :].astype(F32) * (grad_weights - delta)).astype(BF16)
                ds_s[here, :] = ds
                dq_s[here, :] = merge(plan, h, mm(ds, k_s[...]), dq_s[here, :])

            chunks(plan, one_chunk)
            row = (t * plan.per_tile + h) * 3 * HD
            own = slice(h * HD, (h + 1) * HD)
            grad_ref[row + HD : row + 2 * HD, :] = mm(q_t[own, :], ds_s[...]).astype(BF16)
            grad_ref[row + 2 * HD : row + 3 * HD, :] = mm(g_t[own, :], low_ref[head]).astype(BF16)
        dq_t = dq_s[...].T.astype(BF16)
        for h in range(plan.per_tile):
            row = (t * plan.per_tile + h) * 3 * HD
            grad_ref[row : row + HD, :] = dq_t[h * HD : (h + 1) * HD, :]
    if with_weight:
        wgrad_ref[...] = mm(grad_ref[...], full_ref[...]).astype(BF16)


def weight_kernel(plan, grad_ref, full_ref, got_ref, *parts):
    size = parts[0].shape[0]
    for i, part in enumerate(parts):
        here = slice(i * size, (i + 1) * size)
        product = mm(grad_ref[here, :], full_ref[...])
        part[...] = (product + got_ref[here, :].astype(F32)).astype(BF16)


def whole_weight_kernel(plan, grad_ref, full_ref, wgrad_ref):
    wgrad_ref[...] = mm(grad_ref[...], full_ref[...]).astype(BF16)


def term_kernel(plan, slots, *refs):
    which, weight, sum_ref = refs[:3]
    grads = refs[3 : 3 + plan.groups]
    sends = refs[3 + plan.groups :]
    width = weight.shape[1]
    for s, out in zip(slots, sends):
        here = slice(s * plan.rows, (s + 1) * plan.rows)
        total = None
        for i, grad in enumerate(grads):
            if plan.groups > 1:
                group = which[0] if i == 0 else 1 - which[0]
                here_w = pl.ds(pl.multiple_of(group * plan.gcols, plan.gcols), plan.gcols)
            else:
                here_w = slice(None)
            part = mm(grad[:, here], weight[here_w, :], TN)
            total = part if total is None else total + part
        out[:, :width] = total.astype(BF16)
        if out.shape[1] > width:
            out[:, width:] = sum_ref[here, :].astype(BF16)


def scale_kernel(plan, m, places, which, *refs):
    out, staged, sems = refs[-3:]
    parts = refs[-3 - len(places) : -3]
    size = parts[0].shape[0]
    copies = []
    for i, (own, index, count) in enumerate(places):
        side = which[0] if own else 1 - which[0]
        start = pl.multiple_of((side * count + index) * size, size)
        staged[i] = parts[i][...].astype(F32) * (1.0 / m)
        copies.append(pltpu.make_async_copy(staged.at[i], out.at[pl.ds(start, size), :], sems.at[i]))
        copies[-1].start()
    for copy in copies:
        copy.wait()


def scaled(plan, m, core, parts, places, whole=None):
    rows, width = parts[0].shape
    count = len(parts)
    args = [core.reshape(1), *([] if whole is None else [whole]), *parts]
    specs = [SMEM] + [HBM] * (whole is not None) + [VMEM] * count
    return pl.pallas_call(
        functools.partial(scale_kernel, plan, m, places),
        out_shape=array(2 * places[0][2] * rows, width, dtype=F32),
        in_specs=specs,
        out_specs=HBM,
        scratch_shapes=[pltpu.VMEM((count, rows, width), F32), pltpu.SemaphoreType.DMA((count,))],
        input_output_aliases={} if whole is None else {1: 0},
        compiler_params=pltpu.CompilerParams(vmem_limit_bytes=12 * 2**20),
        cost_estimate=pl.CostEstimate(flops=0, bytes_accessed=1 << 20, transcendentals=0),
    )(*args)


def relay_kernel(plan, own, ahead, out):
    wide = own.shape[1]
    width = wide - plan.heads * HD
    out[:, :width] = add(own[:, :width], ahead[:, :width])
    out[:, width:wide] = own[:, width:]
    out[:, wide:] = ahead[:, width:]


def combine_kernel(plan, pieces, place, *refs):
    hcols = plan.heads * HD
    received, (node_grad, attended) = refs[:-2], refs[-2:]
    width = node_grad.shape[1]
    total = received[0][:, :width].astype(F32)
    for x in received[1:]:
        if x.shape[1] >= width:
            total = total + x[:, :width].astype(F32)
    node_grad[...] = total.astype(BF16)
    for slot, (i, at) in enumerate(pieces):
        piece = received[i][:, at : at + hcols]
        if hcols % 128 == 0:
            start = pl.multiple_of((place[0] ^ slot) * hcols, hcols)
            attended[:, pl.ds(start, hcols)] = piece
        else:
            attended[slot, :, :] = piece


def size(x):
    return math.prod(x.shape) * jnp.dtype(x.dtype).itemsize


def call(kernel, plan, out_shape, scratch, flops, args, scalar=False, far=()):
    arrays = [x for x in scratch if hasattr(x, "dtype") and len(x.shape) > 0]
    held = sum(map(size, out_shape)) + sum(map(size, arrays)) + sum(map(size, args))
    held += 32 * plan.chunk * plan.nodes + 24 * plan.nodes * 2 * HD + 8 * 2**20
    return pl.pallas_call(
        functools.partial(kernel, plan),
        out_shape=out_shape,
        in_specs=[
            SMEM if scalar and i == 0 else HBM if i in far else VMEM for i in range(len(args))
        ],
        out_specs=[VMEM] * len(out_shape),
        scratch_shapes=scratch,
        compiler_params=pltpu.CompilerParams(vmem_limit_bytes=min(held, 60 * 2**20)),
        cost_estimate=pl.CostEstimate(flops=flops, bytes_accessed=4 << 20, transcendentals=0),
    )(*args)


def array(*shape, dtype=BF16):
    return jax.ShapeDtypeStruct(shape, dtype)


def swap(x, axis, bits):
    size = lax.axis_size(axis)
    return lax.ppermute(x, axis, [(i, i ^ bits) for i in range(size)])


def after(x, *done):
    return lax.optimization_barrier((x, *done))[0]


def add(a, b):
    return (a.astype(F32) + b.astype(F32)).astype(BF16)


def local(node_feats, qkv_weight, block_pairs, grad_out):
    feats = node_feats[0]
    rows, width = feats.shape
    n, m = lax.axis_size("seq"), lax.axis_size("clus")
    z, c = lax.axis_index("seq"), lax.axis_index("clus")
    plan = Plan(rows, qkv_weight.shape[0], n)
    nodes, heads = plan.nodes, plan.heads
    core = c % 2

    hcols = heads * HD

    def for_slot(k):
        return lax.dynamic_slice_in_dim(grad_out[0], (z ^ k) * hcols, hcols, 1)

    qkv_weight, own, mark = call(
        first_kernel,
        plan,
        [array(plan.columns, width), array(rows, plan.columns), array(16, 128)],
        [pltpu.SemaphoreType.DMA(())],
        2 * rows * plan.columns * width,
        [feats, qkv_weight],
        far=(1,),
    )
    if n == 4:
        far, near = swap(feats, "seq", 2), swap(feats, "seq", 1)
        xs = [feats, near, far, jnp.where(z < n, swap(after(far, mark), "seq", 1), near)]
    else:
        xs = [feats] + [swap(feats, "seq", k) for k in range(1, n)]
    earlier = nodes - rows
    (known,) = call(
        project_kernel,
        plan,
        [array(earlier, plan.columns)],
        [],
        2 * earlier * plan.columns * width,
        [own, *xs[-2:0:-1], qkv_weight],
    )

    listed = block_pairs[0]
    always, known = lax.optimization_barrier((listed[0, 0] >= 0, known))
    mine, *sent = after([for_slot(k) for k in range(n)], known)
    grads = [mine] + [swap(sent[k - 1], "seq", k) for k in range(1, n)]

    per_dev = rows // BLOCK
    blocks = nodes // BLOCK
    place = ((listed // per_dev) ^ z) * per_dev + listed % per_dev
    ids = jnp.arange(blocks, dtype=jnp.int32)
    row_ids = jnp.arange(2 * HD, dtype=jnp.int32) % HD
    allowed = jnp.any(
        (place[:, 0, None, None] == row_ids) & (place[:, 1, None, None] == ids[:, None]), axis=0
    )
    blocked = ~allowed & (row_ids < blocks)
    key_bias = jnp.repeat(jnp.where(blocked, NEVER, 0.0).astype(BF16), BLOCK, axis=0)
    row_hot = (jnp.arange(nodes, dtype=jnp.int32)[:, None] // BLOCK == row_ids).astype(BF16)

    def tiles(count):
        return [pltpu.VMEM((nodes, plan.tile), BF16)] * count

    low, sums, full, qkv = call(
        forward_kernel,
        plan,
        [array(heads, nodes, nodes), array(nodes, hcols, dtype=F32), array(nodes, width), array(nodes, plan.columns)],
        tiles(3) + [pltpu.VMEM((nodes, 2 * HD), BF16)],
        4 * nodes * nodes * HD * heads,
        [known, *xs, qkv_weight, key_bias, row_hot],
    )
    scratch = tiles(4) + [pltpu.VMEM((nodes, nodes), BF16), pltpu.VMEM((nodes, plan.tile), F32)]
    flops = 8 * nodes * nodes * HD * plan.gheads
    common = [qkv, *grads, low, sums]
    grad_t = []
    if plan.groups > 1:
        grad_other, wgrad_other = call(
            lambda *a: backward_kernel(a[0], True, *a[1:]),
            plan,
            [array(plan.gcols, nodes), array(plan.gcols, width)],
            scratch,
            flops + 2 * nodes * plan.gcols * width,
            [(1 - core).reshape(1), *common, full],
            scalar=True,
        )
        got = swap(wgrad_other, "clus", 1)
        grad_t = [grad_other]
    (grad_own,) = call(
        lambda *a: backward_kernel(a[0], False, *a[1:]),
        plan,
        [array(plan.gcols, nodes)],
        scratch,
        flops,
        [core.reshape(1), qkv, *grads, low, sums],
        scalar=True,
    )
    grad_t = [grad_own, *grad_t]
    count = 2 * nodes * plan.gcols * width
    half = plan.gcols // 2
    if plan.groups > 1:
        parts = call(
            weight_kernel, plan, [array(half, width)] * 2, [], count, [grad_own, full, got]
        )
    else:
        (wgrad,) = call(
            whole_weight_kernel, plan, [array(plan.gcols, width)], [], count, [grad_own, full]
        )
        keep = lax.dynamic_slice_in_dim(wgrad, core * half, half, 0)
        send = lax.dynamic_slice_in_dim(wgrad, (1 - core) * half, half, 0)
        parts = [add(keep, swap(send, "clus", 1))]
    def terms(slots, wide, *done):
        return call(
            lambda *a: term_kernel(a[0], slots, *a[1:]),
            plan,
            [array(rows, width + hcols * extra) for extra in wide],
            [],
            count * plan.groups * len(slots) // n,
            [core.reshape(1), qkv_weight, after(sums, *done), *grad_t],
            scalar=True,
        )

    if n == 4:
        (ahead,) = terms([3], [1])
        ahead = swap(ahead, "seq", 1)
        own_term, near, far_term = terms([0, 1, 2], [1, 1, 1], parts)
        (pair,) = call(
            relay_kernel, plan, [array(rows, width + 2 * hcols)], [], 0, [far_term, ahead]
        )
        received = [own_term, swap(after(near, ahead), "seq", 1), swap(pair, "seq", 2)]
        places = [(0, width), (1, width), (2, width), (2, width + hcols)]
    else:
        sends = terms(range(n), [1] * n)
        received = [sends[0]] + [swap(sends[k], "seq", k) for k in range(1, n)]
        places = [(k, width) for k in range(n)]

    bits = []
    while 2 << len(bits) < m:
        bits.append(2 << len(bits))

    def across(x, stage):
        pairs = [(i, i ^ (bits[-1 - stage] if i % 2 else bits[stage])) for i in range(m)]
        return lax.ppermute(x, "clus", pairs)

    def finish(parts, gots):
        parts = [add(part, got) for part, got in zip(parts, gots)]
        for stage in range(1, len(bits)):
            gots = [across(part, stage) for part in parts]
            parts = [add(part, got) for part, got in zip(parts, gots)]
        gots = [swap(part, "clus", 1) for part in parts]
        held, places = [], []
        for i, (part, got) in enumerate(zip(parts, gots)):
            held += [part, got]
            places += [(True, i, len(parts)), (False, i, len(parts))]
        result = scaled(plan, m, core, held[:-1], places[:-1])
        result = scaled(plan, m, core, held[-1:], places[-1:], result)
        return result

    gots = [across(part, 0) for part in parts]
    weight_grad = lax.cond(
        always,
        finish,
        lambda parts, gots: jnp.zeros((plan.columns, width), F32),
        parts,
        gots,
    )

    received = after(received, weight_grad)
    aligned = hcols % 128 == 0
    node_grad, attended = call(
        lambda *a: combine_kernel(a[0], places, *a[1:]),
        plan,
        [array(rows, width), array(rows, n * hcols) if aligned else array(n, rows, hcols)],
        [],
        0,
        [z.reshape(1), *received],
        scalar=True,
    )
    if not aligned:
        order = jnp.arange(n, dtype=jnp.int32) ^ z
        attended = attended[order].transpose(1, 0, 2).reshape(rows, n * hcols)
    return (attended[None], node_grad[None], weight_grad)


def solution(mesh):
    return jax.shard_map(
        local,
        mesh=mesh,
        in_specs=(
            P("clus", "seq", None),
            P("seq", None),
            P("clus", None, None),
            P("clus", "seq", None),
        ),
        out_specs=(P("clus", "seq", None), P("clus", "seq", None), P("seq", None)),
        check_vma=False,
    )
```

```python
import functools
import math

import jax
import jax.numpy as jnp
from jax import lax
from jax.experimental import pallas as pl
from jax.experimental.pallas import tpu as pltpu
from jax.sharding import PartitionSpec as P

HD = 64
BLOCK = 128
F32 = jnp.float32
BF16 = jnp.bfloat16
NT = (((1,), (1,)), ((), ()))
TN = (((0,), (0,)), ((), ()))
NEVER = -1e30
VMEM = pl.BlockSpec(memory_space=pltpu.VMEM)
HBM = pl.BlockSpec(memory_space=pltpu.HBM)
SMEM = pl.BlockSpec(memory_space=pltpu.SMEM)


def mm(a, b, dims=(((1,), (0,)), ((), ()))):
    return lax.dot_general(a, b, dims, preferred_element_type=F32)


class Plan:
    def __init__(self, rows, columns, n):
        self.n, self.rows, self.columns = n, rows, columns
        self.nodes = n * rows
        self.heads = columns // (3 * HD)
        self.groups = 2 if self.heads % 2 == 0 else 1
        self.gheads = self.heads // self.groups
        self.pair = self.gheads % 2 == 0
        self.per_tile = 2 if self.pair else 1
        self.tiles = self.gheads // self.per_tile
        self.tile = self.per_tile * HD
        self.gcols = self.gheads * 3 * HD
        self.chunk = math.gcd(self.nodes, 512)

    def base(self, group, t):
        start = group * self.gcols + t * 3 * self.tile
        return start if isinstance(start, int) else pl.multiple_of(start, self.tile)

    def feature(self, group, t):
        start = (group * self.tiles + t) * self.tile
        return start if isinstance(start, int) else pl.multiple_of(start, self.tile)


def low_half(shape):
    return lax.broadcasted_iota(jnp.int32, shape, 1) % (2 * HD) < HD


def first_kernel(plan, x, weight, weight_out, qkv, mark, sem):
    copy = pltpu.make_async_copy(weight, weight_out, sem)
    copy.start()
    copy.wait()
    qkv[...] = mm(x[...], weight_out[...], NT).astype(BF16)
    mark[...] = qkv[: mark.shape[0], : mark.shape[1]]


def project_kernel(plan, *refs):
    own, feats, (weight, qkv) = refs[0], refs[-3:0:-1], refs[-2:]
    qkv[: plan.rows, :] = own[...]
    for s, x in enumerate(feats, 1):
        here = slice(s * plan.rows, (s + 1) * plan.rows)
        qkv[here, :] = mm(x[...], weight[...], NT).astype(BF16)


def load_tile(plan, qkv, group, t, q_s, k_s, v_s):
    base, tile = plan.base(group, t), plan.tile
    for s in range(plan.n):
        here = slice(s * plan.rows, (s + 1) * plan.rows)
        first, second, third = (qkv[here, pl.ds(base + i * tile, tile)] for i in range(3))
        if plan.pair:
            low = low_half(first.shape)
            queries = jnp.where(low, first, second)
            keys = pltpu.roll(jnp.where(low, third, first).astype(F32), HD, 1).astype(BF16)
            values = jnp.where(low, second, third)
        else:
            queries, keys, values = first, second, third
        q_s[here, :] = (queries.astype(F32) * HD ** -0.5).astype(BF16)
        k_s[here, :] = keys
        v_s[here, :] = values


def with_lanes(plan, h, x, extra):
    if not plan.pair:
        return jnp.concatenate([x, extra[:, :HD]], axis=1)
    low = low_half(x.shape)
    return jnp.where(low if h == 0 else ~low, x, extra)


def only_head(plan, h, x):
    if not plan.pair:
        return x
    low = low_half(x.shape)
    return jnp.where(low if h == 0 else ~low, x, jnp.zeros_like(x))


def merge(plan, h, x, before):
    if not plan.pair or h == 0:
        return x
    return jnp.where(low_half(x.shape), before, x)


def chunks(plan, body):
    steps = plan.nodes // plan.chunk
    if steps <= 4:
        for i in range(steps):
            body(i * plan.chunk)
    else:
        def step(i, carry):
            body(pl.multiple_of(i * plan.chunk, plan.chunk))
            return carry

        lax.fori_loop(0, steps, step, 0)


def forward_kernel(plan, *refs):
    n, rows = plan.n, plan.rows
    known, feats, (weight, key_bias, row_hot) = refs[0], refs[1 : 1 + n], refs[1 + n : 4 + n]
    low_ref, sum_ref, full_ref, tiles_ref = refs[4 + n : 8 + n]
    qkv, ka_s = refs[8 + n :]
    for s, x in enumerate(feats):
        full_ref[s * rows : (s + 1) * rows, :] = x[...]
    earlier = (n - 1) * rows
    qkv[:earlier, :] = known[...]
    qkv[earlier:, :] = mm(feats[-1][...], weight[...], NT).astype(BF16)
    for group in range(plan.groups):
        for t in range(plan.tiles):
            tile = group * plan.tiles + t
            q_s, k_s, v_s = (tiles_ref.at[3 * tile + i] for i in range(3))
            load_tile(plan, qkv, group, t, q_s, k_s, v_s)
            lanes = slice(plan.feature(group, t), plan.feature(group, t) + plan.tile)
            for h in range(plan.per_tile):
                head = (group * plan.tiles + t) * plan.per_tile + h
                ka_s[...] = with_lanes(plan, h, k_s[...], key_bias[...])

                def one_chunk(lo):
                    here = pl.ds(lo, plan.chunk)
                    queries = with_lanes(plan, h, q_s[here, :], row_hot[here, :])
                    scores = mm(queries, ka_s[...], NT)
                    unnorm = jnp.exp(scores - jnp.max(scores, axis=-1, keepdims=True))
                    low = (unnorm * (1.0 / jnp.sum(unnorm, axis=-1, keepdims=True))).astype(BF16)
                    low_ref[head, here, :] = low
                    sum_ref[here, lanes] = merge(plan, h, mm(low, v_s[...]), sum_ref[here, lanes])

                chunks(plan, one_chunk)


def backward_kernel(plan, with_weight, *refs):
    n, rows, tile = plan.n, plan.rows, plan.tile
    group = refs[0][0] if plan.groups > 1 else 0
    tiles_ref, grads = refs[1], refs[2 : 2 + n]
    low_ref, sum_ref = refs[2 + n : 4 + n]
    at = 4 + n
    if with_weight:
        full_ref = refs[at]
        at += 1
    grad_ref = refs[at]
    at += 1
    if with_weight:
        wgrad_ref = refs[at]
        at += 1
    k_s, g_s, ds_s, dq_s = refs[at:]
    for t in range(plan.tiles):
        index = 3 * (group * plan.tiles + t)
        q_s, v_s = tiles_ref.at[index], tiles_ref.at[index + 2]
        feature = plan.feature(group, t)
        for s in range(n):
            g_s[s * rows : (s + 1) * rows, :] = grads[s][:, pl.ds(feature, tile)]
        k_s[...] = (tiles_ref[index + 1].astype(F32) * HD ** -0.5).astype(BF16)
        q_t = q_s[...].T
        g_t = g_s[...].T
        for h in range(plan.per_tile):
            head = (group * plan.tiles + t) * plan.per_tile + h

            def one_chunk(lo):
                here = pl.ds(lo, plan.chunk)
                g_here = only_head(plan, h, g_s[here, :])
                delta = jnp.sum(
                    g_here.astype(F32) * sum_ref[here, pl.ds(feature, tile)], axis=-1, keepdims=True
                )
                grad_weights = mm(g_here, v_s[...], NT)
                ds = (low_ref[head, here, :].astype(F32) * (grad_weights - delta)).astype(BF16)
                ds_s[here, :] = ds
                dq_s[here, :] = merge(plan, h, mm(ds, k_s[...]), dq_s[here, :])

            chunks(plan, one_chunk)
            row = (t * plan.per_tile + h) * 3 * HD
            own = slice(h * HD, (h + 1) * HD)
            grad_ref[row + HD : row + 2 * HD, :] = mm(q_t[own, :], ds_s[...]).astype(BF16)
            grad_ref[row + 2 * HD : row + 3 * HD, :] = mm(g_t[own, :], low_ref[head]).astype(BF16)
        dq_t = dq_s[...].T.astype(BF16)
        for h in range(plan.per_tile):
            row = (t * plan.per_tile + h) * 3 * HD
            grad_ref[row : row + HD, :] = dq_t[h * HD : (h + 1) * HD, :]
    if with_weight:
        wgrad_ref[...] = mm(grad_ref[...], full_ref[...]).astype(BF16)


def weight_kernel(plan, grad_ref, full_ref, got_ref, *parts):
    size = parts[0].shape[0]
    for i, part in enumerate(parts):
        here = slice(i * size, (i + 1) * size)
        product = mm(grad_ref[here, :], full_ref[...])
        part[...] = (product + got_ref[here, :].astype(F32)).astype(BF16)


def whole_weight_kernel(plan, grad_ref, full_ref, wgrad_ref):
    wgrad_ref[...] = mm(grad_ref[...], full_ref[...]).astype(BF16)


def term_kernel(plan, slots, *refs):
    which, weight, sum_ref = refs[:3]
    grads = refs[3 : 3 + plan.groups]
    sends = refs[3 + plan.groups :]
    width = weight.shape[1]
    for s, out in zip(slots, sends):
        here = slice(s * plan.rows, (s + 1) * plan.rows)
        total = None
        for i, grad in enumerate(grads):
            if plan.groups > 1:
                group = which[0] if i == 0 else 1 - which[0]
                here_w = pl.ds(pl.multiple_of(group * plan.gcols, plan.gcols), plan.gcols)
            else:
                here_w = slice(None)
            part = mm(grad[:, here], weight[here_w, :], TN)
            total = part if total is None else total + part
        out[:, :width] = total.astype(BF16)
        if out.shape[1] > width:
            out[:, width:] = sum_ref[here, :].astype(BF16)


def scale_kernel(plan, m, places, which, *refs):
    out, staged, sems = refs[-3:]
    parts = refs[-3 - len(places) : -3]
    size = parts[0].shape[0]
    copies = []
    for i, (own, index, count) in enumerate(places):
        side = which[0] if own else 1 - which[0]
        start = pl.multiple_of((side * count + index) * size, size)
        staged[i] = parts[i][...].astype(F32) * (1.0 / m)
        copies.append(pltpu.make_async_copy(staged.at[i], out.at[pl.ds(start, size), :], sems.at[i]))
        copies[-1].start()
    for copy in copies:
        copy.wait()


def scaled(plan, m, core, parts, places, whole=None):
    rows, width = parts[0].shape
    count = len(parts)
    args = [core.reshape(1), *([] if whole is None else [whole]), *parts]
    specs = [SMEM] + [HBM] * (whole is not None) + [VMEM] * count
    return pl.pallas_call(
        functools.partial(scale_kernel, plan, m, places),
        out_shape=array(2 * places[0][2] * rows, width, dtype=F32),
        in_specs=specs,
        out_specs=HBM,
        scratch_shapes=[pltpu.VMEM((count, rows, width), F32), pltpu.SemaphoreType.DMA((count,))],
        input_output_aliases={} if whole is None else {1: 0},
        compiler_params=pltpu.CompilerParams(vmem_limit_bytes=12 * 2**20),
        cost_estimate=pl.CostEstimate(flops=0, bytes_accessed=1 << 20, transcendentals=0),
    )(*args)


def relay_kernel(plan, own, ahead, out):
    wide = own.shape[1]
    width = wide - plan.heads * HD
    out[:, :width] = add(own[:, :width], ahead[:, :width])
    out[:, width:wide] = own[:, width:]
    out[:, wide:] = ahead[:, width:]


def combine_kernel(plan, pieces, place, *refs):
    hcols = plan.heads * HD
    received, (node_grad, attended) = refs[:-2], refs[-2:]
    width = node_grad.shape[1]
    total = received[0][:, :width].astype(F32)
    for x in received[1:]:
        if x.shape[1] >= width:
            total = total + x[:, :width].astype(F32)
    node_grad[...] = total.astype(BF16)
    for slot, (i, at) in enumerate(pieces):
        piece = received[i][:, at : at + hcols]
        if hcols % 128 == 0:
            start = pl.multiple_of((place[0] ^ slot) * hcols, hcols)
            attended[:, pl.ds(start, hcols)] = piece
        else:
            attended[slot, :, :] = piece


def size(x):
    return math.prod(x.shape) * jnp.dtype(x.dtype).itemsize


def call(kernel, plan, out_shape, scratch, flops, args, scalar=False, far=()):
    arrays = [x for x in scratch if hasattr(x, "dtype") and len(x.shape) > 0]
    held = sum(map(size, out_shape)) + sum(map(size, arrays)) + sum(map(size, args))
    held += 32 * plan.chunk * plan.nodes + 24 * plan.nodes * 2 * HD + 8 * 2**20
    return pl.pallas_call(
        functools.partial(kernel, plan),
        out_shape=out_shape,
        in_specs=[
            SMEM if scalar and i == 0 else HBM if i in far else VMEM for i in range(len(args))
        ],
        out_specs=[VMEM] * len(out_shape),
        scratch_shapes=scratch,
        compiler_params=pltpu.CompilerParams(vmem_limit_bytes=min(held, 60 * 2**20)),
        cost_estimate=pl.CostEstimate(flops=flops, bytes_accessed=4 << 20, transcendentals=0),
    )(*args)


def array(*shape, dtype=BF16):
    return jax.ShapeDtypeStruct(shape, dtype)


def swap(x, axis, bits):
    size = lax.axis_size(axis)
    return lax.ppermute(x, axis, [(i, i ^ bits) for i in range(size)])


def after(x, *done):
    return lax.optimization_barrier((x, *done))[0]


def add(a, b):
    return (a.astype(F32) + b.astype(F32)).astype(BF16)


def local(node_feats, qkv_weight, block_pairs, grad_out):
    feats = node_feats[0]
    rows, width = feats.shape
    n, m = lax.axis_size("seq"), lax.axis_size("clus")
    z, c = lax.axis_index("seq"), lax.axis_index("clus")
    plan = Plan(rows, qkv_weight.shape[0], n)
    nodes, heads = plan.nodes, plan.heads
    core = c % 2

    hcols = heads * HD

    def for_slot(k):
        return lax.dynamic_slice_in_dim(grad_out[0], (z ^ k) * hcols, hcols, 1)

    qkv_weight, own, mark = call(
        first_kernel,
        plan,
        [array(plan.columns, width), array(rows, plan.columns), array(16, 128)],
        [pltpu.SemaphoreType.DMA(())],
        2 * rows * plan.columns * width,
        [feats, qkv_weight],
        far=(1,),
    )
    if n == 4:
        far, near = swap(feats, "seq", 2), swap(feats, "seq", 1)
        xs = [feats, near, far, jnp.where(z < n, swap(after(far, mark), "seq", 1), near)]
    else:
        xs = [feats] + [swap(feats, "seq", k) for k in range(1, n)]
    earlier = nodes - rows
    (known,) = call(
        project_kernel,
        plan,
        [array(earlier, plan.columns)],
        [],
        2 * earlier * plan.columns * width,
        [own, *xs[-2:0:-1], qkv_weight],
    )

    listed = block_pairs[0]
    always, known = lax.optimization_barrier((listed[0, 0] >= 0, known))
    mine, *sent = after([for_slot(k) for k in range(n)], known)
    grads = [mine] + [swap(sent[k - 1], "seq", k) for k in range(1, n)]

    per_dev = rows // BLOCK
    blocks = nodes // BLOCK
    place = ((listed // per_dev) ^ z) * per_dev + listed % per_dev
    ids = jnp.arange(blocks, dtype=jnp.int32)
    row_ids = jnp.arange(2 * HD, dtype=jnp.int32) % HD
    allowed = jnp.any(
        (place[:, 0, None, None] == row_ids) & (place[:, 1, None, None] == ids[:, None]), axis=0
    )
    blocked = ~allowed & (row_ids < blocks)
    key_bias = jnp.repeat(jnp.where(blocked, NEVER, 0.0).astype(BF16), BLOCK, axis=0)
    row_hot = (jnp.arange(nodes, dtype=jnp.int32)[:, None] // BLOCK == row_ids).astype(BF16)

    def tiles(count):
        return [pltpu.VMEM((nodes, plan.tile), BF16)] * count

    low, sums, full, projected = call(
        forward_kernel,
        plan,
        [array(heads, nodes, nodes), array(nodes, hcols, dtype=F32), array(nodes, width)]
        + [array(3 * heads // plan.per_tile, nodes, plan.tile)],
        [pltpu.VMEM((nodes, plan.columns), BF16), pltpu.VMEM((nodes, 2 * HD), BF16)],
        4 * nodes * nodes * HD * heads,
        [known, *xs, qkv_weight, key_bias, row_hot],
    )
    scratch = tiles(2) + [pltpu.VMEM((nodes, nodes), BF16), pltpu.VMEM((nodes, plan.tile), F32)]
    flops = 8 * nodes * nodes * HD * plan.gheads
    common = [projected, *grads, low, sums]
    grad_t = []
    if plan.groups > 1:
        grad_other, wgrad_other = call(
            lambda *a: backward_kernel(a[0], True, *a[1:]),
            plan,
            [array(plan.gcols, nodes), array(plan.gcols, width)],
            scratch,
            flops + 2 * nodes * plan.gcols * width,
            [(1 - core).reshape(1), *common, full],
            scalar=True,
        )
        got = swap(wgrad_other, "clus", 1)
        grad_t = [grad_other]
    (grad_own,) = call(
        lambda *a: backward_kernel(a[0], False, *a[1:]),
        plan,
        [array(plan.gcols, nodes)],
        scratch,
        flops,
        [core.reshape(1), projected, *grads, low, sums],
        scalar=True,
    )
    grad_t = [grad_own, *grad_t]
    count = 2 * nodes * plan.gcols * width
    half = plan.gcols // 2
    if plan.groups > 1:
        parts = call(
            weight_kernel, plan, [array(half, width)] * 2, [], count, [grad_own, full, got]
        )
    else:
        (wgrad,) = call(
            whole_weight_kernel, plan, [array(plan.gcols, width)], [], count, [grad_own, full]
        )
        keep = lax.dynamic_slice_in_dim(wgrad, core * half, half, 0)
        send = lax.dynamic_slice_in_dim(wgrad, (1 - core) * half, half, 0)
        parts = [add(keep, swap(send, "clus", 1))]
    def terms(slots, wide, *done):
        return call(
            lambda *a: term_kernel(a[0], slots, *a[1:]),
            plan,
            [array(rows, width + hcols * extra) for extra in wide],
            [],
            count * plan.groups * len(slots) // n,
            [core.reshape(1), qkv_weight, after(sums, *done), *grad_t],
            scalar=True,
        )

    if n == 4:
        (ahead,) = terms([3], [1])
        ahead = swap(ahead, "seq", 1)
        own_term, near, far_term = terms([0, 1, 2], [1, 1, 1], parts)
        (pair,) = call(
            relay_kernel, plan, [array(rows, width + 2 * hcols)], [], 0, [far_term, ahead]
        )
        received = [own_term, swap(after(near, ahead), "seq", 1), swap(pair, "seq", 2)]
        places = [(0, width), (1, width), (2, width), (2, width + hcols)]
    else:
        sends = terms(range(n), [1] * n)
        received = [sends[0]] + [swap(sends[k], "seq", k) for k in range(1, n)]
        places = [(k, width) for k in range(n)]

    bits = []
    while 2 << len(bits) < m:
        bits.append(2 << len(bits))

    def across(x, stage):
        pairs = [(i, i ^ (bits[-1 - stage] if i % 2 else bits[stage])) for i in range(m)]
        return lax.ppermute(x, "clus", pairs)

    def finish(parts, gots):
        parts = [add(part, got) for part, got in zip(parts, gots)]
        for stage in range(1, len(bits)):
            gots = [across(part, stage) for part in parts]
            parts = [add(part, got) for part, got in zip(parts, gots)]
        gots = [swap(part, "clus", 1) for part in parts]
        held, places = [], []
        for i, (part, got) in enumerate(zip(parts, gots)):
            held += [part, got]
            places += [(True, i, len(parts)), (False, i, len(parts))]
        result = scaled(plan, m, core, held[:-1], places[:-1])
        result = scaled(plan, m, core, held[-1:], places[-1:], result)
        return result

    gots = [across(part, 0) for part in parts]
    weight_grad = lax.cond(
        always,
        finish,
        lambda parts, gots: jnp.zeros((plan.columns, width), F32),
        parts,
        gots,
    )

    received = after(received, weight_grad)
    aligned = hcols % 128 == 0
    node_grad, attended = call(
        lambda *a: combine_kernel(a[0], places, *a[1:]),
        plan,
        [array(rows, width), array(rows, n * hcols) if aligned else array(n, rows, hcols)],
        [],
        0,
        [z.reshape(1), *received],
        scalar=True,
    )
    if not aligned:
        order = jnp.arange(n, dtype=jnp.int32) ^ z
        attended = attended[order].transpose(1, 0, 2).reshape(rows, n * hcols)
    return (attended[None], node_grad[None], weight_grad)


def solution(mesh):
    return jax.shard_map(
        local,
        mesh=mesh,
        in_specs=(
            P("clus", "seq", None),
            P("seq", None),
            P("clus", None, None),
            P("clus", "seq", None),
        ),
        out_specs=(P("clus", "seq", None), P("clus", "seq", None), P("seq", None)),
        check_vma=False,
    )
```
